512 devices in a mesh: gx: 64 (over y, z), gy: 8 (over x, core).
Axes of the slice: x: 4, y: 8, z: 8, core: 2. Of those that a mesh axis runs over, the one named last changes fastest.
Arguments:
- right_border: float32 [5, 64, 128, 256], P(None, 'gx', 'gy'), may hold values from -8 to 8
- left_border: float32 [5, 64, 128, 256], P(None, 'gx', 'gy'), may hold values from -8 to 8
- velocity: float32 [3, 64, 128, 256], P(None, 'gx', 'gy'), may hold values from -5 to 5
- reaction: float32 [5, 64, 128, 256], P(None, 'gx', 'gy'), may hold values from 0.5 to 4
- diffusivity: float32 [5], replicated, may hold values from 0.5 to 2
- coupling: float32 [5, 5], replicated, may hold values from -3 to 3
Outputs:
- right_vector: float32 [5, 64, 128, 256], P(None, 'gx', 'gy')
- left_vector: float32 [5, 64, 128, 256], P(None, 'gx', 'gy')
The draws below stay inside these ranges and needn't reach their ends.
All inputs are finite; a program needn't handle non-finite values.
Results may differ from the reference program's by a relative error of at most 0.0029.
Values sent between devices are 32-bit elements; how exact they have to be, the bound alone decides.
No kernel may reach another device: no remote copies, remote signals or barrier semaphores. Data moves between devices by JAX's collectives and lax.ppermute only.
A program may use at most 64 MiB of HBM per device.

```python
import math
import jax
import jax.numpy as jnp
from jax import lax

COMPS = 5
NZ = 256
ITERS = 2
NX = 64
NY = 128


def levels(key, dims, pieces, smallest, top_value):
    def one(axis_at, blocks):
        heights = jax.random.uniform(jax.random.fold_in(jax.random.fold_in(key, 6), axis_at), (blocks,), jnp.float32, smallest / len(pieces), top_value / len(pieces))
        return jnp.repeat(jnp.exp(heights), dims[axis_at] // blocks).reshape((-1,) + (1,) * (len(dims) - axis_at - 1))

    factor_of = one(*pieces[0])
    for cut in pieces[1:]:
        factor_of = factor_of * one(*cut)
    return factor_of


def bell_draw(rng, extent, deviation, most, pieces=(), kind=jnp.bfloat16):
    level = levels(rng, extent, pieces, -0.22, 0.18) if pieces else 1.0
    entries = jax.random.normal(rng, extent, jnp.float32) * deviation * level
    return jnp.minimum(jnp.maximum(entries, -most), most).astype(kind)


def setup_inputs(seed: int = 0) -> dict:
    streams_of = jax.random.split(jax.random.key(seed), 7)
    return {
        "right_border": bell_draw(streams_of[0], (COMPS, NX, NY, NZ), 1.0, 8.0, ((1, 64), (2, 8)), jnp.float32),
        "left_border": bell_draw(streams_of[1], (COMPS, NX, NY, NZ), 1.0, 8.0, ((1, 64), (2, 8)), jnp.float32),
        "velocity": bell_draw(streams_of[2], (3, NX, NY, NZ), 1.0, 5.0, ((1, 64), (2, 8)), jnp.float32),
        "reaction": jnp.clip(jnp.exp(math.log(4.0) - 2.0794415 * jax.random.uniform(streams_of[3], (COMPS, NX, NY, NZ), jnp.float32) ** levels(streams_of[3], (COMPS, NX, NY, NZ), ((1, 64), (2, 8)), -0.2, 0.2)), 0.5, 4.0),
        "diffusivity": jnp.clip(jnp.exp(jax.random.uniform(streams_of[4], (COMPS,), jnp.float32, math.log(0.5), math.log(2.0))), 0.5, 2.0),
        "coupling": bell_draw(streams_of[5], (COMPS, COMPS), 0.5, 3.0, (), jnp.float32),
    }


CENTER = 8.0 / 3.0
EDGE = -1.0 / 6.0
CORNER = -1.0 / 12.0

def add_depth(vec_field):
    return jnp.pad(vec_field, ((0, 0), (0, 0), (0, 0), (1, 1)))

def beside_all(extended, shift_x, shift_y, shift_z):
    return extended[:, 1 + shift_x:extended.shape[1] - 1 + shift_x, 1 + shift_y:extended.shape[2] - 1 + shift_y, 1 + shift_z:extended.shape[3] - 1 + shift_z]

def laplace(extended):
    summed = CENTER * beside_all(extended, 0, 0, 0)
    for shift_x in (-1, 0, 1):
        for shift_y in (-1, 0, 1):
            for shift_z in (-1, 0, 1):
                offsets = abs(shift_x) + abs(shift_y) + abs(shift_z)
                if offsets == 2:
                    summed = summed + EDGE * beside_all(extended, shift_x, shift_y, shift_z)
                elif offsets == 3:
                    summed = summed + CORNER * beside_all(extended, shift_x, shift_y, shift_z)
    return summed

def forward_local(extended, velocity, reaction, diffusivity, coupling):
    center = beside_all(extended, 0, 0, 0)
    result = diffusivity[:, None, None, None] * laplace(extended)
    drift_sum = velocity[0:1] * (beside_all(extended, 1, 0, 0) - beside_all(extended, -1, 0, 0))
    drift_sum = drift_sum + velocity[1:2] * (beside_all(extended, 0, 1, 0) - beside_all(extended, 0, -1, 0))
    drift_sum = drift_sum + velocity[2:3] * (beside_all(extended, 0, 0, 1) - beside_all(extended, 0, 0, -1))
    mixing = jnp.einsum('cd,dxyz->cxyz', coupling, center, precision=lax.Precision.HIGHEST)
    return result + 0.5 * drift_sum + reaction * center + mixing

def adjoint_local(extended, flux_x, flux_y, flux_z, reaction, diffusivity, coupling):
    center = beside_all(extended, 0, 0, 0)
    result = diffusivity[:, None, None, None] * laplace(extended)
    drift_sum = beside_all(flux_x, 1, 0, 0) - beside_all(flux_x, -1, 0, 0)
    drift_sum = drift_sum + (beside_all(flux_y, 0, 1, 0) - beside_all(flux_y, 0, -1, 0))
    drift_sum = drift_sum + (flux_z[:, :, :, 2:] - flux_z[:, :, :, :-2])
    mixing = jnp.einsum('dc,dxyz->cxyz', coupling, center, precision=lax.Precision.HIGHEST)
    return result - 0.5 * drift_sum + reaction * center + mixing

def wrap_ext(vec_field):
    return add_depth(jnp.pad(vec_field, ((0, 0), (1, 1), (1, 1), (0, 0)), mode='wrap'))

def solve_small(start_len, columns):
    column_count = len(columns)
    hessenberg = jnp.zeros((column_count + 1, column_count), jnp.float32)
    for column, (coeffs, length) in enumerate(columns):
        hessenberg = hessenberg.at[:column + 1, column].set(coeffs)
        hessenberg = hessenberg.at[column + 1, column].set(length)
    normal = jnp.dot(hessenberg.T, hessenberg, precision=lax.Precision.HIGHEST)
    target = start_len * hessenberg[0]
    rows_list = [normal[row] for row in range(column_count)]
    rhs_list = [target[row] for row in range(column_count)]
    for pivot in range(column_count):
        for lower in range(pivot + 1, column_count):
            factor = rows_list[lower][pivot] / rows_list[pivot][pivot]
            rows_list[lower] = rows_list[lower] - factor * rows_list[pivot]
            rhs_list[lower] = rhs_list[lower] - factor * rhs_list[pivot]
    answer = [None] * column_count
    for pivot in range(column_count - 1, -1, -1):
        summed = rhs_list[pivot]
        for upper in range(pivot + 1, column_count):
            summed = summed - rows_list[pivot][upper] * answer[upper]
        answer[pivot] = summed / rows_list[pivot][pivot]
    return answer

def krylov(first_vec, apply_fn):
    start_len = jnp.sqrt(jnp.sum(first_vec * first_vec))
    krylov_basis = [first_vec / start_len]
    columns = []
    for iteration in range(ITERS):
        mapped = apply_fn(krylov_basis[-1])
        coeffs = jnp.stack([jnp.sum(member * mapped) for member in krylov_basis])
        for member_pos in range(len(krylov_basis)):
            mapped = mapped - coeffs[member_pos] * krylov_basis[member_pos]
        length = jnp.sqrt(jnp.sum(mapped * mapped))
        columns.append((coeffs, length))
        krylov_basis.append(mapped / length)
    answer = solve_small(start_len, columns)
    result = answer[0] * krylov_basis[0]
    for column in range(1, ITERS):
        result = result + answer[column] * krylov_basis[column]
    return result

def reference(right_border, left_border, velocity, reaction, diffusivity, coupling):

    def forward_apply(vec_field):
        return forward_local(wrap_ext(vec_field), velocity, reaction, diffusivity, coupling)

    def adjoint_apply(vec_field):
        flux_x = wrap_ext(velocity[0:1] * vec_field)
        flux_y = wrap_ext(velocity[1:2] * vec_field)
        flux_z = add_depth(velocity[2:3] * vec_field)
        return adjoint_local(wrap_ext(vec_field), flux_x, flux_y, flux_z, reaction, diffusivity, coupling)
    right_vector = krylov(right_border, forward_apply)
    left_vector = krylov(left_border, adjoint_apply)
    return (right_vector, left_vector)
```

```python
import functools

import jax
import jax.numpy as jnp
from jax import lax
from jax.experimental import pallas as pl
from jax.experimental.pallas import tpu as pltpu
from jax.sharding import PartitionSpec as P

CENTER = 8.0 / 3.0
EDGE = -1.0 / 6.0

COMPS = 5
FIELDS = 2 * COMPS
SUMS = 5


def up(v):
    size = v.shape[-1]
    lane = lax.broadcasted_iota(jnp.int32, v.shape, v.ndim - 1)
    return jnp.where(lane == size - 1, 0.0, pltpu.roll(v, size - 1, v.ndim - 1))


def down(v):
    lane = lax.broadcasted_iota(jnp.int32, v.shape, v.ndim - 1)
    return jnp.where(lane == 0, 0.0, pltpu.roll(v, 1, v.ndim - 1))


def apply_both(rows, mid, even, odd, sign, vx, vy3, vz, vx_even, vx_odd, react, diff_ref, coup_ref):
    outs = []
    centers = [mid(f, 0) for f in range(FIELDS)]
    for f in range(FIELDS):
        c = f % COMPS
        right = f < COMPS
        b1, b0, b2 = centers[f], mid(f, -1), mid(f, 1)
        e1, o1 = even(f, 0), odd(f, 0)
        ya = (even(f, -1) + odd(f, -1)) + (even(f, 1) + odd(f, 1))
        t = (e1 + o1) + (b0 + b2) + 0.5 * ya
        d = diff_ref[c]
        base = (CENTER * d + react(c)) * b1
        if right:
            drift = (sign * vx) * (e1 - o1) + vy3[1] * (b2 - b0) + vz * (up(b1) - down(b1))
            out = base + (EDGE * d) * (ya + up(t) + down(t)) + 0.5 * drift
            for k in range(COMPS):
                out = out + coup_ref[c, k] * centers[k]
        else:
            fz = 0.5 * (vz * b1)
            g = (EDGE * d) * t
            drift = sign * (vx_even * e1 - vx_odd * o1) + (vy3[2] * b2 - vy3[0] * b0)
            out = base + (EDGE * d) * ya - 0.5 * drift + up(g - fz) + down(g + fz)
            for k in range(COMPS):
                out = out + coup_ref[k, c] * centers[COMPS + k]
        outs.append(out)
    return outs


def sign_here():
    return jnp.where(lax.rem(lax.axis_index("gx"), 2) == 0, 1.0, -1.0).astype(jnp.float32)


def first_kernel(ny, coup_ref, diff_ref, sr, sl, vel, rea, lo, hi, even, odd, out, field, coef):
    rows = ny + 8
    for f in range(FIELDS):
        src = sr if f < COMPS else sl
        field[0, f, 2 : ny + 2] = src[f % COMPS]
        field[0, f, 0:2] = lo[2 * f : 2 * f + 2]
        field[0, f, ny + 2 : ny + 4] = hi[2 * f : 2 * f + 2]
        for side, ref in ((1, even), (2, odd)):
            field[side, f, 2 : ny + 2] = ref[f * ny : (f + 1) * ny]
            at = FIELDS * ny + ny + 2 * f
            field[side, f, 0:2] = ref[at : at + 2]
            at = at + 2 * FIELDS
            field[side, f, ny + 2 : ny + 4] = ref[at : at + 2]
    halo = 2 * FIELDS
    for c in range(COMPS):
        coef[c, 1 : ny + 1] = rea[c]
        coef[c, 0:1] = lo[halo + c : halo + c + 1]
        coef[c, ny + 1 : ny + 2] = hi[halo + c : halo + c + 1]
    halo += COMPS
    for at, k, row in ((5, 0, halo), (6, 2, halo + 1)):
        coef[at, 1 : ny + 1] = vel[k]
        coef[at, 0:1] = lo[row : row + 1]
        coef[at, ny + 1 : ny + 2] = hi[row : row + 1]
    for at, ref in ((7, even), (8, odd)):
        coef[at, 1 : ny + 1] = ref[FIELDS * ny : FIELDS * ny + ny]
        last = FIELDS * ny + ny + 4 * FIELDS
        coef[at, 0:1] = ref[last : last + 1]
        coef[at, ny + 1 : ny + 2] = ref[last + 1 : last + 2]
    coef[9, 2 : ny + 2] = vel[1]
    coef[9, 0:2] = lo[halo + 2 : halo + 4]
    coef[9, ny + 2 : ny + 4] = hi[halo + 2 : halo + 4]

    def plane(side):
        return lambda f, shift: field[side, f, 1 + shift : 1 + shift + rows]

    outs = apply_both(
        rows, plane(0), plane(1), plane(2), sign_here(),
        coef[5, 0:rows], [coef[9, k : k + rows] for k in range(3)], coef[6, 0:rows],
        coef[7, 0:rows], coef[8, 0:rows], lambda c: coef[c, 0:rows], diff_ref, coup_ref,
    )
    for f in range(FIELDS):
        field[0, f, 0:rows] = outs[f]
        out[f * ny : (f + 1) * ny] = field[0, f, 1 : ny + 1]
        at = FIELDS * ny + 2 * f
        out[at : at + 1] = field[0, f, 0:1]
        out[at + 1 : at + 2] = field[0, f, ny + 1 : ny + 2]


def second_kernel(ny, copies, coup_ref, diff_ref, sr, sl, vel, rea, lo, hi, even1, odd1, own, even, odd, out, field, vys):
    for f in range(FIELDS):
        for side, ref in ((0, own), (1, even), (2, odd)):
            field[side, f, 1 : ny + 1] = ref[f * ny : (f + 1) * ny]
            at = FIELDS * ny + 2 * f
            field[side, f, 0:1] = ref[at : at + 1]
            field[side, f, ny + 1 : ny + 2] = ref[at + 1 : at + 2]
    row = 2 * FIELDS + COMPS + 2
    vys[1 : ny + 1] = vel[1]
    vys[0:1] = lo[row + 1 : row + 2]
    vys[ny + 1 : ny + 2] = hi[row : row + 1]

    def plane(side):
        return lambda f, shift: field[side, f, 1 + shift : 1 + shift + ny]

    at = FIELDS * ny
    outs = apply_both(
        ny, plane(0), plane(1), plane(2), sign_here(),
        vel[0], [vys[k : k + ny] for k in range(3)], vel[2],
        even1[at : at + ny], odd1[at : at + ny], lambda c: rea[c], diff_ref, coup_ref,
    )
    lane = lax.broadcasted_iota(jnp.int32, (1, 128), 1)
    total = jnp.zeros((1, 128), jnp.float32)
    for system, start in ((0, sr), (1, sl)):
        sums = [0.0] * SUMS
        for c in range(COMPS):
            f = system * COMPS + c
            s, w1, w2 = start[c], field[0, f, 1 : ny + 1], outs[f]
            for k, term in enumerate((w1 * w1, w1 * w2, w2 * w2, w1 * s, w2 * s)):
                sums[k] = sums[k] + term
        for k in range(SUMS):
            value = jnp.sum(jnp.sum(sums[k], axis=0, keepdims=True), axis=1, keepdims=True)
            total = total + jnp.where(lane == system * SUMS + k, value, 0.0)
    out[...] = jnp.broadcast_to(total, (copies, 128))


def last_kernel(ny, parts, sr, sl, own, out_r, out_l):
    total = jnp.sum(parts[...], axis=0, keepdims=True)
    lane = lax.broadcasted_iota(jnp.int32, (1, 128), 1)
    for system, start, out in ((0, sr, out_r), (1, sl, out_l)):
        g11, g12, g22, r1, r2 = [
            jnp.sum(jnp.where(lane == system * SUMS + k, total, 0.0), axis=1, keepdims=True)
            for k in range(SUMS)
        ]
        factor = g12 / g11
        b = (r2 - factor * r1) / (g22 - factor * g12)
        a = (r1 - g12 * b) / g11
        for c in range(COMPS):
            f = system * COMPS + c
            out[c] = a * start[c] + b * own[f * ny : (f + 1) * ny]


def per_device(right_border, left_border, velocity, reaction, diffusivity, coupling):
    comps, _, ny, nz = right_border.shape
    nx_count, ny_count = lax.axis_size("gx"), lax.axis_size("gy")
    f32 = jnp.float32
    sr, sl, vel, rea = (v.reshape(v.shape[0], ny, nz) for v in (right_border, left_border, velocity, reaction))

    def edge(two, one):
        pick = lambda v, where: v[..., where, :].reshape(-1, nz)
        return jnp.concatenate(
            [pick(sr, two), pick(sl, two), pick(rea, one), pick(vel[0:1], one), pick(vel[2:3], one), pick(vel[1:2], two)]
        )

    ahead = [(i, (i + 1) % ny_count) for i in range(ny_count)]
    back = [(j, i) for i, j in ahead]
    lo = lax.ppermute(edge(slice(ny - 2, ny), slice(ny - 1, ny)), "gy", ahead)
    hi = lax.ppermute(edge(slice(0, 2), slice(0, 1)), "gy", back)

    even_pairs = [(i, i ^ 1) for i in range(nx_count)]
    odd_pairs = [(i, (i - 1 if i % 2 == 0 else i + 1) % nx_count) for i in range(nx_count)]

    def swap(v):
        return lax.ppermute(v, "gx", even_pairs), lax.ppermute(v, "gx", odd_pairs)

    halo, vx_row = 2 * FIELDS, 2 * FIELDS + COMPS
    payload = jnp.concatenate(
        [
            sr.reshape(-1, nz), sl.reshape(-1, nz), vel[0], lo[:halo], hi[:halo],
            lo[vx_row : vx_row + 1], hi[vx_row : vx_row + 1],
        ]
    )
    even1, odd1 = swap(payload)

    smem, vmem = pl.BlockSpec(memory_space=pltpu.SMEM), pl.BlockSpec(memory_space=pltpu.VMEM)
    own = pl.pallas_call(
        functools.partial(first_kernel, ny),
        out_shape=jax.ShapeDtypeStruct((FIELDS * (ny + 2), nz), f32),
        in_specs=[smem] * 2 + [vmem] * 8,
        out_specs=vmem,
        scratch_shapes=[pltpu.VMEM((3, FIELDS, ny + 16, nz), f32), pltpu.VMEM((10, ny + 16, nz), f32)],
        name="first_product",
    )(coupling, diffusivity, sr, sl, vel, rea, lo, hi, even1, odd1)
    even2, odd2 = swap(own)
    shares = pl.pallas_call(
        functools.partial(second_kernel, ny, ny_count),
        out_shape=jax.ShapeDtypeStruct((ny_count, 128), f32),
        in_specs=[smem] * 2 + [vmem] * 11,
        out_specs=vmem,
        scratch_shapes=[pltpu.VMEM((3, FIELDS, ny + 8, nz), f32), pltpu.VMEM((ny + 8, nz), f32)],
        name="second_product",
    )(coupling, diffusivity, sr, sl, vel, rea, lo, hi, even1, odd1, own, even2, odd2)
    shares = lax.all_to_all(shares, "gy", 0, 0, tiled=True)
    shares = jnp.broadcast_to(jnp.sum(shares, axis=0, keepdims=True), (nx_count, 128))
    shares = lax.all_to_all(shares, "gx", 0, 0, tiled=True)
    right, left = pl.pallas_call(
        functools.partial(last_kernel, ny),
        out_shape=[jax.ShapeDtypeStruct((comps, ny, nz), f32)] * 2,
        in_specs=[vmem] * 4,
        out_specs=[vmem] * 2,
        name="combine",
    )(shares, sr, sl, own)
    return right.reshape(right_border.shape), left.reshape(left_border.shape)


def solution(mesh):
    block = P(None, "gx", "gy", None)
    return jax.shard_map(
        per_device,
        mesh=mesh,
        in_specs=(block, block, block, block, P(), P()),
        out_specs=(block, block),
        check_vma=False,
    )
```

```python
import functools

import jax
import jax.numpy as jnp
from jax import lax
from jax.experimental import pallas as pl
from jax.experimental.pallas import tpu as pltpu
from jax.sharding import PartitionSpec as P

CENTER = 8.0 / 3.0
EDGE = -1.0 / 6.0

COMPS = 5
FIELDS = 2 * COMPS
SUMS = 5


def up(v):
    size = v.shape[-1]
    lane = lax.broadcasted_iota(jnp.int32, v.shape, v.ndim - 1)
    return jnp.where(lane == size - 1, 0.0, pltpu.roll(v, size - 1, v.ndim - 1))


def down(v):
    lane = lax.broadcasted_iota(jnp.int32, v.shape, v.ndim - 1)
    return jnp.where(lane == 0, 0.0, pltpu.roll(v, 1, v.ndim - 1))


def apply_both(mid, even, odd, sign, vx, vy3, vz, vx_even, vx_odd, react, diff_ref, coup_ref):
    outs = []
    centers = [mid(f, 0) for f in range(FIELDS)]
    for f in range(FIELDS):
        c = f % COMPS
        right = f < COMPS
        b1, b0, b2 = centers[f], mid(f, -1), mid(f, 1)
        e1, o1 = even(f, 0), odd(f, 0)
        ya = (even(f, -1) + odd(f, -1)) + (even(f, 1) + odd(f, 1))
        t = (e1 + o1) + (b0 + b2) + 0.5 * ya
        d = diff_ref[c]
        base = (CENTER * d + react(c)) * b1
        if right:
            drift = (sign * vx) * (e1 - o1) + vy3[1] * (b2 - b0) + vz * (up(b1) - down(b1))
            out = base + (EDGE * d) * (ya + up(t) + down(t)) + 0.5 * drift
            for k in range(COMPS):
                out = out + coup_ref[c, k] * centers[k]
        else:
            fz = 0.5 * (vz * b1)
            g = (EDGE * d) * t
            drift = sign * (vx_even * e1 - vx_odd * o1) + (vy3[2] * b2 - vy3[0] * b0)
            out = base + (EDGE * d) * ya - 0.5 * drift + up(g - fz) + down(g + fz)
            for k in range(COMPS):
                out = out + coup_ref[k, c] * centers[COMPS + k]
        outs.append(out)
    return outs


def in_vmem(*arrays):
    return [pltpu.with_memory_space_constraint(v, pltpu.VMEM) for v in arrays]


def in_hbm(*arrays):
    return [pltpu.with_memory_space_constraint(v, pltpu.HBM) for v in arrays]


def in_smem(*arrays):
    return [pltpu.with_memory_space_constraint(v, pltpu.SMEM) for v in arrays]


def sign_here():
    return jnp.where(lax.rem(lax.axis_index("gx"), 2) == 0, 1.0, -1.0).astype(jnp.float32)


def load_kernel(ny, sr, sl, vel, rea, base, coef, low, high, sems):
    half = COMPS * ny
    copies = [
        pltpu.make_async_copy(src, dst, sems.at[k])
        for k, (src, dst) in enumerate(
            (
                (sr, base.at[0:half]),
                (sl, base.at[half : 2 * half]),
                (vel.at[0:ny], base.at[2 * half : 2 * half + ny]),
                (rea, coef.at[0:half]),
                (vel.at[ny : 3 * ny], coef.at[half : half + 2 * ny]),
            )
        )
    ]
    for copy in copies:
        copy.start()
    for copy in copies:
        copy.wait()
    for out, two, one in ((low, 0, 0), (high, ny - 2, ny - 1)):
        for f in range(FIELDS):
            out[2 * f : 2 * f + 2] = base[f * ny + two : f * ny + two + 2]
        row = 2 * FIELDS
        for c in range(COMPS):
            out[row + c : row + c + 1] = coef[c * ny + one : c * ny + one + 1]
        row += COMPS
        at = half + ny + one
        out[row : row + 1] = coef[at : at + 1]
        at = half + two
        out[row + 1 : row + 3] = coef[at : at + 2]
        at = 2 * half + one
        out[row + 3 : row + 4] = base[at : at + 1]


def fill_kernel(ny, base_in, coef_in, lo, hi, base, coef):
    del base_in, coef_in
    wide, thin = 2 * FIELDS, COMPS + 3
    at, last = (FIELDS + 1) * ny, (FIELDS + 1) * ny + 2 * wide
    base[at : at + wide] = lo[0:wide]
    base[at + wide : last] = hi[0:wide]
    base[last : last + 1] = lo[wide + thin : wide + thin + 1]
    base[last + 1 : last + 2] = hi[wide + thin : wide + thin + 1]
    at = (COMPS + 2) * ny
    coef[at : at + thin] = lo[wide : wide + thin]
    coef[at + thin : at + 2 * thin] = hi[wide : wide + thin]


def first_kernel(ny, coup_ref, diff_ref, base, coef, even, odd, out, field, cext):
    rows = ny + 8
    for f in range(FIELDS):
        for side, ref in ((0, base), (1, even), (2, odd)):
            field[side, f, 2 : ny + 2] = ref[f * ny : (f + 1) * ny]
            at = (FIELDS + 1) * ny + 2 * f
            field[side, f, 0:2] = ref[at : at + 2]
            at = at + 2 * FIELDS
            field[side, f, ny + 2 : ny + 4] = ref[at : at + 2]
    lo, hi = (COMPS + 2) * ny, (COMPS + 2) * ny + COMPS + 3
    for c in range(COMPS + 1):
        at = c * ny if c < COMPS else (COMPS + 1) * ny
        cext[c, 1 : ny + 1] = coef[at : at + ny]
        cext[c, 0:1] = coef[lo + c : lo + c + 1]
        cext[c, ny + 1 : ny + 2] = coef[hi + c : hi + c + 1]
    at, last = FIELDS * ny, (FIELDS + 1) * ny + 4 * FIELDS
    for k, ref in ((6, base), (7, even), (8, odd)):
        cext[k, 1 : ny + 1] = ref[at : at + ny]
        cext[k, 0:1] = ref[last : last + 1]
        cext[k, ny + 1 : ny + 2] = ref[last + 1 : last + 2]
    cext[9, 2 : ny + 2] = coef[COMPS * ny : (COMPS + 1) * ny]
    cext[9, 0:2] = coef[lo + COMPS + 1 : lo + COMPS + 3]
    cext[9, ny + 2 : ny + 4] = coef[hi + COMPS + 1 : hi + COMPS + 3]

    def plane(side):
        return lambda f, shift: field[side, f, 1 + shift : 1 + shift + rows]

    outs = apply_both(
        plane(0), plane(1), plane(2), sign_here(),
        cext[6, 0:rows], [cext[9, k : k + rows] for k in range(3)], cext[5, 0:rows],
        cext[7, 0:rows], cext[8, 0:rows], lambda c: cext[c, 0:rows], diff_ref, coup_ref,
    )
    for f in range(FIELDS):
        field[0, f, 0:rows] = outs[f]
        out[f * ny : (f + 1) * ny] = field[0, f, 1 : ny + 1]
        at = FIELDS * ny + 2 * f
        out[at : at + 1] = field[0, f, 0:1]
        out[at + 1 : at + 2] = field[0, f, ny + 1 : ny + 2]


def second_kernel(ny, copies, coup_ref, diff_ref, base, coef, even1, odd1, own, even, odd, out, field, vys):
    for f in range(FIELDS):
        for side, ref in ((0, own), (1, even), (2, odd)):
            field[side, f, 1 : ny + 1] = ref[f * ny : (f + 1) * ny]
            at = FIELDS * ny + 2 * f
            field[side, f, 0:1] = ref[at : at + 1]
            field[side, f, ny + 1 : ny + 2] = ref[at + 1 : at + 2]
    row = (COMPS + 2) * ny + COMPS + 2
    vys[1 : ny + 1] = coef[COMPS * ny : (COMPS + 1) * ny]
    vys[0:1] = coef[row : row + 1]
    row += COMPS + 2
    vys[ny + 1 : ny + 2] = coef[row : row + 1]

    def plane(side):
        return lambda f, shift: field[side, f, 1 + shift : 1 + shift + ny]

    at, vz = FIELDS * ny, (COMPS + 1) * ny
    outs = apply_both(
        plane(0), plane(1), plane(2), sign_here(),
        base[at : at + ny], [vys[k : k + ny] for k in range(3)], coef[vz : vz + ny],
        even1[at : at + ny], odd1[at : at + ny], lambda c: coef[c * ny : (c + 1) * ny], diff_ref, coup_ref,
    )
    lane = lax.broadcasted_iota(jnp.int32, (1, 128), 1)
    total = jnp.zeros((1, 128), jnp.float32)
    for system in range(2):
        sums = [0.0] * SUMS
        for f in range(system * COMPS, (system + 1) * COMPS):
            s, w1, w2 = base[f * ny : (f + 1) * ny], field[0, f, 1 : ny + 1], outs[f]
            for k, term in enumerate((w1 * w1, w1 * w2, w2 * w2, w1 * s, w2 * s)):
                sums[k] = sums[k] + term
        for k in range(SUMS):
            value = jnp.sum(jnp.sum(sums[k], axis=0, keepdims=True), axis=1, keepdims=True)
            total = total + jnp.where(lane == system * SUMS + k, value, 0.0)
    out[...] = jnp.broadcast_to(total, (copies, 128))


def last_kernel(ny, parts, base, own, out_r, out_l):
    total = jnp.sum(parts[...], axis=0, keepdims=True)
    lane = lax.broadcasted_iota(jnp.int32, (1, 128), 1)
    for system, out in ((0, out_r), (1, out_l)):
        g11, g12, g22, r1, r2 = [
            jnp.sum(jnp.where(lane == system * SUMS + k, total, 0.0), axis=1, keepdims=True)
            for k in range(SUMS)
        ]
        factor = g12 / g11
        b = (r2 - factor * r1) / (g22 - factor * g12)
        a = (r1 - g12 * b) / g11
        at = system * COMPS * ny
        out[...] = a * base[at : at + COMPS * ny] + b * own[at : at + COMPS * ny]


def per_device(right_border, left_border, velocity, reaction, diffusivity, coupling):
    comps, _, ny, nz = right_border.shape
    nx_count, ny_count = lax.axis_size("gx"), lax.axis_size("gy")
    f32 = jnp.float32
    params = pltpu.CompilerParams(vmem_limit_bytes=16 * 1024 * 1024)
    smem, vmem = pl.BlockSpec(memory_space=pltpu.SMEM), pl.BlockSpec(memory_space=pltpu.VMEM)
    sr, sl, vel, rea = (v.reshape(-1, nz) for v in (right_border, left_border, velocity, reaction))

    base_rows, coef_rows = (FIELDS + 1) * ny + 4 * FIELDS + 2, (COMPS + 2) * ny + 2 * (COMPS + 3)
    edge_rows = 2 * FIELDS + COMPS + 4
    base, coef, low, high = pl.pallas_call(
        functools.partial(load_kernel, ny),
        out_shape=[pltpu.VMEM((rows, nz), f32) for rows in (base_rows, coef_rows, edge_rows, edge_rows)],
        in_specs=[pl.BlockSpec(memory_space=pltpu.HBM)] * 4,
        out_specs=[vmem] * 4,
        scratch_shapes=[pltpu.SemaphoreType.DMA((5,))],
        compiler_params=params,
        name="load",
    )(*in_hbm(sr, sl, vel, rea))

    ahead = [(i, (i + 1) % ny_count) for i in range(ny_count)]
    back = [(j, i) for i, j in ahead]
    lo = lax.ppermute(high, "gy", ahead)
    hi = lax.ppermute(low, "gy", back)
    base, coef = pl.pallas_call(
        functools.partial(fill_kernel, ny),
        out_shape=[pltpu.VMEM(base.shape, f32), pltpu.VMEM(coef.shape, f32)],
        in_specs=[vmem] * 4,
        out_specs=[vmem] * 2,
        input_output_aliases={0: 0, 1: 1},
        compiler_params=params,
        name="fill",
    )(*in_vmem(base, coef, lo, hi))

    even_pairs = [(i, i ^ 1) for i in range(nx_count)]
    odd_pairs = [(i, (i - 1 if i % 2 == 0 else i + 1) % nx_count) for i in range(nx_count)]

    def swap(v):
        odd = lax.ppermute(v, "gx", odd_pairs)
        return lax.ppermute(v, "gx", even_pairs), odd

    even1, odd1 = swap(base)
    scalars = in_smem(coupling, diffusivity)
    own = pl.pallas_call(
        functools.partial(first_kernel, ny),
        out_shape=pltpu.VMEM((FIELDS * (ny + 2), nz), f32),
        in_specs=[smem] * 2 + [vmem] * 4,
        out_specs=vmem,
        scratch_shapes=[pltpu.VMEM((3, FIELDS, ny + 16, nz), f32), pltpu.VMEM((10, ny + 16, nz), f32)],
        compiler_params=params,
        name="first_product",
    )(*scalars, *in_vmem(base, coef, even1, odd1))
    even2, odd2 = swap(own)
    shares = pl.pallas_call(
        functools.partial(second_kernel, ny, ny_count),
        out_shape=pltpu.VMEM((ny_count, 128), f32),
        in_specs=[smem] * 2 + [vmem] * 7,
        out_specs=vmem,
        scratch_shapes=[pltpu.VMEM((3, FIELDS, ny + 8, nz), f32), pltpu.VMEM((ny + 8, nz), f32)],
        compiler_params=params,
        name="second_product",
    )(*scalars, *in_vmem(base, coef, even1, odd1, own, even2, odd2))
    shares = lax.all_to_all(shares, "gy", 0, 0, tiled=True)
    shares = jnp.broadcast_to(jnp.sum(shares, axis=0, keepdims=True), (nx_count, 128))
    shares = lax.all_to_all(shares, "gx", 0, 0, tiled=True)
    right, left = pl.pallas_call(
        functools.partial(last_kernel, ny),
        out_shape=[jax.ShapeDtypeStruct((comps * ny, nz), f32)] * 2,
        in_specs=[vmem] * 3,
        out_specs=[vmem] * 2,
        compiler_params=params,
        name="combine",
    )(*in_vmem(shares, base, own))
    return right.reshape(right_border.shape), left.reshape(left_border.shape)


def solution(mesh):
    block = P(None, "gx", "gy", None)
    return jax.shard_map(
        per_device,
        mesh=mesh,
        in_specs=(block, block, block, block, P(), P()),
        out_specs=(block, block),
        check_vma=False,
    )
```

```python
import functools

import jax
import jax.numpy as jnp
from jax import lax
from jax.experimental import pallas as pl
from jax.experimental.pallas import tpu as pltpu
from jax.sharding import PartitionSpec as P

CENTER = 8.0 / 3.0
EDGE = -1.0 / 6.0

COMPS = 5
FIELDS = 2 * COMPS
SUMS = 5


def up(v):
    size = v.shape[-1]
    lane = lax.broadcasted_iota(jnp.int32, v.shape, v.ndim - 1)
    return jnp.where(lane == size - 1, 0.0, pltpu.roll(v, size - 1, v.ndim - 1))


def down(v):
    lane = lax.broadcasted_iota(jnp.int32, v.shape, v.ndim - 1)
    return jnp.where(lane == 0, 0.0, pltpu.roll(v, 1, v.ndim - 1))


def apply_both(mid, even, odd, vx, vy3, vz, vx_even, vx_odd, react, scal):
    number = lambda k: scal[k : k + 1]
    sign = number(COMPS * COMPS + COMPS)
    outs = []
    centers = [mid(f, 0) for f in range(FIELDS)]
    for f in range(FIELDS):
        c = f % COMPS
        right = f < COMPS
        b1, b0, b2 = centers[f], mid(f, -1), mid(f, 1)
        e1, o1 = even(f, 0), odd(f, 0)
        ya = (even(f, -1) + odd(f, -1)) + (even(f, 1) + odd(f, 1))
        t = (e1 + o1) + (b0 + b2) + 0.5 * ya
        d = number(COMPS * COMPS + c)
        base = (CENTER * d + react(c)) * b1
        if right:
            drift = (sign * vx) * (e1 - o1) + vy3[1] * (b2 - b0) + vz * (up(b1) - down(b1))
            out = base + (EDGE * d) * (ya + up(t) + down(t)) + 0.5 * drift
            for k in range(COMPS):
                out = out + number(c * COMPS + k) * centers[k]
        else:
            fz = 0.5 * (vz * b1)
            g = (EDGE * d) * t
            drift = sign * (vx_even * e1 - vx_odd * o1) + (vy3[2] * b2 - vy3[0] * b0)
            out = base + (EDGE * d) * ya - 0.5 * drift + up(g - fz) + down(g + fz)
            for k in range(COMPS):
                out = out + number(k * COMPS + c) * centers[COMPS + k]
        outs.append(out)
    return outs


def in_vmem(*arrays):
    return [pltpu.with_memory_space_constraint(v, pltpu.VMEM) for v in arrays]


def in_hbm(*arrays):
    return [pltpu.with_memory_space_constraint(v, pltpu.HBM) for v in arrays]


def numbers_kernel(coup_ref, diff_ref, scal):
    for k in range(COMPS * COMPS):
        scal[k : k + 1] = jnp.full((1, scal.shape[1]), coup_ref[k // COMPS, k % COMPS], jnp.float32)
    for c in range(COMPS):
        scal[COMPS * COMPS + c : COMPS * COMPS + c + 1] = jnp.full((1, scal.shape[1]), diff_ref[c], jnp.float32)
    sign = jnp.where(lax.rem(lax.axis_index("gx"), 2) == 0, 1.0, -1.0).astype(jnp.float32)
    last = COMPS * COMPS + COMPS
    scal[last : last + 1] = jnp.full((1, scal.shape[1]), sign, jnp.float32)


def load_kernel(ny, sr, sl, vel, rea, base, coef, low, high, sems):
    half = COMPS * ny
    copies = [
        pltpu.make_async_copy(src, dst, sems.at[k])
        for k, (src, dst) in enumerate(
            (
                (sr, base.at[0:half]),
                (sl, base.at[half : 2 * half]),
                (vel.at[0:ny], base.at[2 * half : 2 * half + ny]),
                (rea, coef.at[0:half]),
                (vel.at[ny : 3 * ny], coef.at[half : half + 2 * ny]),
            )
        )
    ]
    for copy in copies:
        copy.start()
    for copy in copies:
        copy.wait()
    for out, two, one in ((low, 0, 0), (high, ny - 2, ny - 1)):
        for f in range(FIELDS):
            out[2 * f : 2 * f + 2] = base[f * ny + two : f * ny + two + 2]
        row = 2 * FIELDS
        for c in range(COMPS):
            out[row + c : row + c + 1] = coef[c * ny + one : c * ny + one + 1]
        row += COMPS
        at = half + ny + one
        out[row : row + 1] = coef[at : at + 1]
        at = half + two
        out[row + 1 : row + 3] = coef[at : at + 2]
        at = 2 * half + one
        out[row + 3 : row + 4] = base[at : at + 1]


def fill_kernel(ny, base_in, coef_in, lo, hi, base, coef):
    del base_in, coef_in
    wide, thin = 2 * FIELDS, COMPS + 3
    at, last = (FIELDS + 1) * ny, (FIELDS + 1) * ny + 2 * wide
    base[at : at + wide] = lo[0:wide]
    base[at + wide : last] = hi[0:wide]
    base[last : last + 1] = lo[wide + thin : wide + thin + 1]
    base[last + 1 : last + 2] = hi[wide + thin : wide + thin + 1]
    at = (COMPS + 2) * ny
    coef[at : at + thin] = lo[wide : wide + thin]
    coef[at + thin : at + 2 * thin] = hi[wide : wide + thin]


def first_kernel(ny, scal, base, coef, even, odd, out, field, cext):
    rows = ny + 8
    for f in range(FIELDS):
        for side, ref in ((0, base), (1, even), (2, odd)):
            field[side, f, 2 : ny + 2] = ref[f * ny : (f + 1) * ny]
            at = (FIELDS + 1) * ny + 2 * f
            field[side, f, 0:2] = ref[at : at + 2]
            at = at + 2 * FIELDS
            field[side, f, ny + 2 : ny + 4] = ref[at : at + 2]
    lo, hi = (COMPS + 2) * ny, (COMPS + 2) * ny + COMPS + 3
    for c in range(COMPS + 1):
        at = c * ny if c < COMPS else (COMPS + 1) * ny
        cext[c, 1 : ny + 1] = coef[at : at + ny]
        cext[c, 0:1] = coef[lo + c : lo + c + 1]
        cext[c, ny + 1 : ny + 2] = coef[hi + c : hi + c + 1]
    at, last = FIELDS * ny, (FIELDS + 1) * ny + 4 * FIELDS
    for k, ref in ((6, base), (7, even), (8, odd)):
        cext[k, 1 : ny + 1] = ref[at : at + ny]
        cext[k, 0:1] = ref[last : last + 1]
        cext[k, ny + 1 : ny + 2] = ref[last + 1 : last + 2]
    cext[9, 2 : ny + 2] = coef[COMPS * ny : (COMPS + 1) * ny]
    cext[9, 0:2] = coef[lo + COMPS + 1 : lo + COMPS + 3]
    cext[9, ny + 2 : ny + 4] = coef[hi + COMPS + 1 : hi + COMPS + 3]

    def plane(side):
        return lambda f, shift: field[side, f, 1 + shift : 1 + shift + rows]

    outs = apply_both(
        plane(0), plane(1), plane(2),
        cext[6, 0:rows], [cext[9, k : k + rows] for k in range(3)], cext[5, 0:rows],
        cext[7, 0:rows], cext[8, 0:rows], lambda c: cext[c, 0:rows], scal,
    )
    for f in range(FIELDS):
        field[0, f, 0:rows] = outs[f]
        out[f * ny : (f + 1) * ny] = field[0, f, 1 : ny + 1]
        at = FIELDS * ny + 2 * f
        out[at : at + 1] = field[0, f, 0:1]
        out[at + 1 : at + 2] = field[0, f, ny + 1 : ny + 2]


def second_kernel(ny, copies, scal, base, coef, even1, odd1, own, even, odd, out, field, vys):
    for f in range(FIELDS):
        for side, ref in ((0, own), (1, even), (2, odd)):
            field[side, f, 1 : ny + 1] = ref[f * ny : (f + 1) * ny]
            at = FIELDS * ny + 2 * f
            field[side, f, 0:1] = ref[at : at + 1]
            field[side, f, ny + 1 : ny + 2] = ref[at + 1 : at + 2]
    row = (COMPS + 2) * ny + COMPS + 2
    vys[1 : ny + 1] = coef[COMPS * ny : (COMPS + 1) * ny]
    vys[0:1] = coef[row : row + 1]
    row += COMPS + 2
    vys[ny + 1 : ny + 2] = coef[row : row + 1]

    def plane(side):
        return lambda f, shift: field[side, f, 1 + shift : 1 + shift + ny]

    at, vz = FIELDS * ny, (COMPS + 1) * ny
    outs = apply_both(
        plane(0), plane(1), plane(2),
        base[at : at + ny], [vys[k : k + ny] for k in range(3)], coef[vz : vz + ny],
        even1[at : at + ny], odd1[at : at + ny], lambda c: coef[c * ny : (c + 1) * ny], scal,
    )
    lane = lax.broadcasted_iota(jnp.int32, (1, 128), 1)
    total = jnp.zeros((1, 128), jnp.float32)
    for system in range(2):
        sums = [0.0] * SUMS
        for f in range(system * COMPS, (system + 1) * COMPS):
            s, w1, w2 = base[f * ny : (f + 1) * ny], field[0, f, 1 : ny + 1], outs[f]
            for k, term in enumerate((w1 * w1, w1 * w2, w2 * w2, w1 * s, w2 * s)):
                sums[k] = sums[k] + term
        for k in range(SUMS):
            value = jnp.sum(jnp.sum(sums[k], axis=0, keepdims=True), axis=1, keepdims=True)
            total = total + jnp.where(lane == system * SUMS + k, value, 0.0)
    out[...] = jnp.broadcast_to(total, (copies, 128))


def last_kernel(ny, parts, base, own, out_r, out_l):
    total = jnp.sum(parts[...], axis=0, keepdims=True)
    lane = lax.broadcasted_iota(jnp.int32, (1, 128), 1)
    for system, out in ((0, out_r), (1, out_l)):
        g11, g12, g22, r1, r2 = [
            jnp.sum(jnp.where(lane == system * SUMS + k, total, 0.0), axis=1, keepdims=True)
            for k in range(SUMS)
        ]
        factor = g12 / g11
        b = (r2 - factor * r1) / (g22 - factor * g12)
        a = (r1 - g12 * b) / g11
        at = system * COMPS * ny
        out[...] = a * base[at : at + COMPS * ny] + b * own[at : at + COMPS * ny]


def per_device(right_border, left_border, velocity, reaction, diffusivity, coupling):
    comps, _, ny, nz = right_border.shape
    nx_count, ny_count = lax.axis_size("gx"), lax.axis_size("gy")
    f32 = jnp.float32
    params = pltpu.CompilerParams(vmem_limit_bytes=16 * 1024 * 1024)
    smem, vmem = pl.BlockSpec(memory_space=pltpu.SMEM), pl.BlockSpec(memory_space=pltpu.VMEM)
    sr, sl, vel, rea = (v.reshape(-1, nz) for v in (right_border, left_border, velocity, reaction))

    base_rows, coef_rows = (FIELDS + 1) * ny + 4 * FIELDS + 2, (COMPS + 2) * ny + 2 * (COMPS + 3)
    edge_rows = 2 * FIELDS + COMPS + 4
    base, coef, low, high = pl.pallas_call(
        functools.partial(load_kernel, ny),
        out_shape=[pltpu.VMEM((rows, nz), f32) for rows in (base_rows, coef_rows, edge_rows, edge_rows)],
        in_specs=[pl.BlockSpec(memory_space=pltpu.HBM)] * 4,
        out_specs=[vmem] * 4,
        scratch_shapes=[pltpu.SemaphoreType.DMA((5,))],
        compiler_params=params,
        name="load",
    )(*in_hbm(sr, sl, vel, rea))

    scal = pl.pallas_call(
        numbers_kernel,
        out_shape=pltpu.VMEM((32, nz), f32),
        in_specs=[smem] * 2,
        out_specs=vmem,
        compiler_params=params,
        name="numbers",
    )(coupling, diffusivity)

    ahead = [(i, (i + 1) % ny_count) for i in range(ny_count)]
    back = [(j, i) for i, j in ahead]
    lo = lax.ppermute(high, "gy", ahead)
    hi = lax.ppermute(low, "gy", back)
    base, coef = pl.pallas_call(
        functools.partial(fill_kernel, ny),
        out_shape=[pltpu.VMEM(base.shape, f32), pltpu.VMEM(coef.shape, f32)],
        in_specs=[vmem] * 4,
        out_specs=[vmem] * 2,
        input_output_aliases={0: 0, 1: 1},
        compiler_params=params,
        name="fill",
    )(*in_vmem(base, coef, lo, hi))

    even_pairs = [(i, i ^ 1) for i in range(nx_count)]
    odd_pairs = [(i, (i - 1 if i % 2 == 0 else i + 1) % nx_count) for i in range(nx_count)]

    def swap(v):
        odd = lax.ppermute(v, "gx", odd_pairs)
        return lax.ppermute(v, "gx", even_pairs), odd

    even1, odd1 = swap(base)
    own = pl.pallas_call(
        functools.partial(first_kernel, ny),
        out_shape=pltpu.VMEM((FIELDS * (ny + 2), nz), f32),
        in_specs=[vmem] * 5,
        out_specs=vmem,
        scratch_shapes=[pltpu.VMEM((3, FIELDS, ny + 16, nz), f32), pltpu.VMEM((10, ny + 16, nz), f32)],
        compiler_params=params,
        name="first_product",
    )(*in_vmem(scal, base, coef, even1, odd1))
    even2, odd2 = swap(own)
    shares = pl.pallas_call(
        functools.partial(second_kernel, ny, ny_count),
        out_shape=pltpu.VMEM((ny_count, 128), f32),
        in_specs=[vmem] * 8,
        out_specs=vmem,
        scratch_shapes=[pltpu.VMEM((3, FIELDS, ny + 8, nz), f32), pltpu.VMEM((ny + 8, nz), f32)],
        compiler_params=params,
        name="second_product",
    )(*in_vmem(scal, base, coef, even1, odd1, own, even2, odd2))
    shares = lax.all_to_all(shares, "gy", 0, 0, tiled=True)
    shares = jnp.broadcast_to(jnp.sum(shares, axis=0, keepdims=True), (nx_count, 128))
    shares = lax.all_to_all(shares, "gx", 0, 0, tiled=True)
    right, left = pl.pallas_call(
        functools.partial(last_kernel, ny),
        out_shape=[jax.ShapeDtypeStruct((comps * ny, nz), f32)] * 2,
        in_specs=[vmem] * 3,
        out_specs=[vmem] * 2,
        compiler_params=params,
        name="combine",
    )(*in_vmem(shares, base, own))
    return right.reshape(right_border.shape), left.reshape(left_border.shape)


def solution(mesh):
    block = P(None, "gx", "gy", None)
    return jax.shard_map(
        per_device,
        mesh=mesh,
        in_specs=(block, block, block, block, P(), P()),
        out_specs=(block, block),
        check_vma=False,
    )
```

```python
import functools

import jax
import jax.numpy as jnp
from jax import lax
from jax.experimental import pallas as pl
from jax.experimental.pallas import tpu as pltpu
from jax.sharding import PartitionSpec as P

CENTER = 8.0 / 3.0
EDGE = -1.0 / 6.0

COMPS = 5
FIELDS = 2 * COMPS
PLANE_ROWS = 2 * FIELDS + 1
SUMS = 5


def up(v):
    size = v.shape[-1]
    lane = lax.broadcasted_iota(jnp.int32, v.shape, v.ndim - 1)
    return jnp.where(lane == size - 1, 0.0, pltpu.roll(v, size - 1, v.ndim - 1))


def down(v):
    lane = lax.broadcasted_iota(jnp.int32, v.shape, v.ndim - 1)
    return jnp.where(lane == 0, 0.0, pltpu.roll(v, 1, v.ndim - 1))


def apply_both(mid, even, odd, vx, vy3, vz, vx_even, vx_odd, react, scal):
    number = lambda k: scal[k : k + 1]
    sign = number(COMPS * COMPS + COMPS)
    outs = []
    centers = [mid(f, 0) for f in range(FIELDS)]
    for f in range(FIELDS):
        c = f % COMPS
        right = f < COMPS
        b1, b0, b2 = centers[f], mid(f, -1), mid(f, 1)
        e1, o1 = even(f, 0), odd(f, 0)
        ya = (even(f, -1) + odd(f, -1)) + (even(f, 1) + odd(f, 1))
        t = (e1 + o1) + (b0 + b2) + 0.5 * ya
        d = number(COMPS * COMPS + c)
        base = (CENTER * d + react(c)) * b1
        if right:
            drift = (sign * vx) * (e1 - o1) + vy3[1] * (b2 - b0) + vz * (up(b1) - down(b1))
            out = base + (EDGE * d) * (ya + up(t) + down(t)) + 0.5 * drift
            for k in range(COMPS):
                out = out + number(c * COMPS + k) * centers[k]
        else:
            fz = 0.5 * (vz * b1)
            g = (EDGE * d) * t
            drift = sign * (vx_even * e1 - vx_odd * o1) + (vy3[2] * b2 - vy3[0] * b0)
            out = base + (EDGE * d) * ya - 0.5 * drift + up(g - fz) + down(g + fz)
            for k in range(COMPS):
                out = out + number(k * COMPS + c) * centers[COMPS + k]
        outs.append(out)
    return outs


def in_vmem(*arrays):
    return [pltpu.with_memory_space_constraint(v, pltpu.VMEM) for v in arrays]


def in_hbm(*arrays):
    return [pltpu.with_memory_space_constraint(v, pltpu.HBM) for v in arrays]


def numbers_kernel(coup_ref, diff_ref, scal):
    for k in range(COMPS * COMPS):
        scal[k : k + 1] = jnp.full((1, scal.shape[1]), coup_ref[k // COMPS, k % COMPS], jnp.float32)
    for c in range(COMPS):
        scal[COMPS * COMPS + c : COMPS * COMPS + c + 1] = jnp.full((1, scal.shape[1]), diff_ref[c], jnp.float32)
    sign = jnp.where(lax.rem(lax.axis_index("gx"), 2) == 0, 1.0, -1.0).astype(jnp.float32)
    last = COMPS * COMPS + COMPS
    scal[last : last + 1] = jnp.full((1, scal.shape[1]), sign, jnp.float32)


def load_kernel(ny, sr, sl, vel, rea, base, coef, sems):
    half = COMPS * ny
    copies = [
        pltpu.make_async_copy(src, dst, sems.at[k])
        for k, (src, dst) in enumerate(
            (
                (sr, base.at[0:half]),
                (sl, base.at[half : 2 * half]),
                (vel.at[0:ny], base.at[2 * half : 2 * half + ny]),
                (rea, coef.at[0:half]),
                (vel.at[ny : 3 * ny], coef.at[half : half + 2 * ny]),
            )
        )
    ]
    for copy in copies:
        copy.start()
    for copy in copies:
        copy.wait()


def edges_kernel(ny, base, even, odd, coef, low, high):
    for out, two, one in ((low, 0, 0), (high, ny - 2, ny - 1)):
        for plane, ref in enumerate((base, even, odd)):
            row = plane * PLANE_ROWS
            for f in range(FIELDS):
                out[row + 2 * f : row + 2 * f + 2] = ref[f * ny + two : f * ny + two + 2]
            at = FIELDS * ny + one
            out[row + 2 * FIELDS : row + 2 * FIELDS + 1] = ref[at : at + 1]
        row = 3 * PLANE_ROWS
        for c in range(COMPS + 1):
            at = (c if c < COMPS else COMPS + 1) * ny + one
            out[row + c : row + c + 1] = coef[at : at + 1]
        at = COMPS * ny + two
        out[row + COMPS + 1 : row + COMPS + 3] = coef[at : at + 2]


def first_kernel(ny, scal, coef, lo, hi, base, even, odd, out, field, cext):
    rows = ny + 8
    for side, ref in enumerate((base, even, odd)):
        at = side * PLANE_ROWS
        for f in range(FIELDS):
            field[side, f, 2 : ny + 2] = ref[f * ny : (f + 1) * ny]
            field[side, f, 0:2] = lo[at + 2 * f : at + 2 * f + 2]
            field[side, f, ny + 2 : ny + 4] = hi[at + 2 * f : at + 2 * f + 2]
    for c in range(9):
        if c < COMPS + 1:
            at, ref, row = (c if c < COMPS else COMPS + 1) * ny, coef, 3 * PLANE_ROWS + c
        else:
            at, ref, row = FIELDS * ny, (base, even, odd)[c - COMPS - 1], (c - COMPS) * PLANE_ROWS - 1
        cext[c, 1 : ny + 1] = ref[at : at + ny]
        cext[c, 0:1] = lo[row : row + 1]
        cext[c, ny + 1 : ny + 2] = hi[row : row + 1]
    row = 3 * PLANE_ROWS + COMPS + 1
    cext[9, 2 : ny + 2] = coef[COMPS * ny : (COMPS + 1) * ny]
    cext[9, 0:2] = lo[row : row + 2]
    cext[9, ny + 2 : ny + 4] = hi[row : row + 2]

    def plane(side):
        return lambda f, shift: field[side, f, 1 + shift : 1 + shift + rows]

    outs = apply_both(
        plane(0), plane(1), plane(2),
        cext[6, 0:rows], [cext[9, k : k + rows] for k in range(3)], cext[5, 0:rows],
        cext[7, 0:rows], cext[8, 0:rows], lambda c: cext[c, 0:rows], scal,
    )
    for f in range(FIELDS):
        field[0, f, 0:rows] = outs[f]
        out[f * ny : (f + 1) * ny] = field[0, f, 1 : ny + 1]
        at = FIELDS * ny + 2 * f
        out[at : at + 1] = field[0, f, 0:1]
        out[at + 1 : at + 2] = field[0, f, ny + 1 : ny + 2]


def second_kernel(ny, copies, scal, coef, lo, hi, base, even1, odd1, own, even, odd, out, field, vys):
    for f in range(FIELDS):
        for side, ref in ((0, own), (1, even), (2, odd)):
            field[side, f, 1 : ny + 1] = ref[f * ny : (f + 1) * ny]
            at = FIELDS * ny + 2 * f
            field[side, f, 0:1] = ref[at : at + 1]
            field[side, f, ny + 1 : ny + 2] = ref[at + 1 : at + 2]
    row = 3 * PLANE_ROWS + COMPS + 1
    vys[1 : ny + 1] = coef[COMPS * ny : (COMPS + 1) * ny]
    vys[0:1] = lo[row + 1 : row + 2]
    vys[ny + 1 : ny + 2] = hi[row : row + 1]

    def plane(side):
        return lambda f, shift: field[side, f, 1 + shift : 1 + shift + ny]

    at, vz = FIELDS * ny, (COMPS + 1) * ny
    outs = apply_both(
        plane(0), plane(1), plane(2),
        base[at : at + ny], [vys[k : k + ny] for k in range(3)], coef[vz : vz + ny],
        even1[at : at + ny], odd1[at : at + ny], lambda c: coef[c * ny : (c + 1) * ny], scal,
    )
    lane = lax.broadcasted_iota(jnp.int32, (1, 128), 1)
    total = jnp.zeros((1, 128), jnp.float32)
    for system in range(2):
        sums = [0.0] * SUMS
        for f in range(system * COMPS, (system + 1) * COMPS):
            s, w1, w2 = base[f * ny : (f + 1) * ny], field[0, f, 1 : ny + 1], outs[f]
            for k, term in enumerate((w1 * w1, w1 * w2, w2 * w2, w1 * s, w2 * s)):
                sums[k] = sums[k] + term
        for k in range(SUMS):
            value = jnp.sum(jnp.sum(sums[k], axis=0, keepdims=True), axis=1, keepdims=True)
            total = total + jnp.where(lane == system * SUMS + k, value, 0.0)
    out[...] = jnp.broadcast_to(total, (copies, 128))


def last_kernel(ny, parts, base, own, out_r, out_l):
    total = jnp.sum(parts[...], axis=0, keepdims=True)
    lane = lax.broadcasted_iota(jnp.int32, (1, 128), 1)
    for system, out in ((0, out_r), (1, out_l)):
        g11, g12, g22, r1, r2 = [
            jnp.sum(jnp.where(lane == system * SUMS + k, total, 0.0), axis=1, keepdims=True)
            for k in range(SUMS)
        ]
        factor = g12 / g11
        b = (r2 - factor * r1) / (g22 - factor * g12)
        a = (r1 - g12 * b) / g11
        at = system * COMPS * ny
        out[...] = a * base[at : at + COMPS * ny] + b * own[at : at + COMPS * ny]


def per_device(right_border, left_border, velocity, reaction, diffusivity, coupling):
    comps, _, ny, nz = right_border.shape
    nx_count, ny_count = lax.axis_size("gx"), lax.axis_size("gy")
    f32 = jnp.float32
    params = pltpu.CompilerParams(vmem_limit_bytes=16 * 1024 * 1024)
    smem, vmem = pl.BlockSpec(memory_space=pltpu.SMEM), pl.BlockSpec(memory_space=pltpu.VMEM)
    sr, sl, vel, rea = (v.reshape(-1, nz) for v in (right_border, left_border, velocity, reaction))

    base, coef = pl.pallas_call(
        functools.partial(load_kernel, ny),
        out_shape=[pltpu.VMEM((rows * ny, nz), f32) for rows in (FIELDS + 1, COMPS + 2)],
        in_specs=[pl.BlockSpec(memory_space=pltpu.HBM)] * 4,
        out_specs=[vmem] * 2,
        scratch_shapes=[pltpu.SemaphoreType.DMA((5,))],
        compiler_params=params,
        name="load",
    )(*in_hbm(sr, sl, vel, rea))
    scal = pl.pallas_call(
        numbers_kernel,
        out_shape=pltpu.VMEM((32, nz), f32),
        in_specs=[smem] * 2,
        out_specs=vmem,
        compiler_params=params,
        name="numbers",
    )(coupling, diffusivity)

    even_pairs = [(i, i ^ 1) for i in range(nx_count)]
    odd_pairs = [(i, (i - 1 if i % 2 == 0 else i + 1) % nx_count) for i in range(nx_count)]

    def swap(v):
        odd = lax.ppermute(v, "gx", odd_pairs)
        return lax.ppermute(v, "gx", even_pairs), odd

    even1, odd1 = swap(base)
    low, high = pl.pallas_call(
        functools.partial(edges_kernel, ny),
        out_shape=[pltpu.VMEM((-(-(3 * PLANE_ROWS + COMPS + 3) // 8) * 8, nz), f32)] * 2,
        in_specs=[vmem] * 4,
        out_specs=[vmem] * 2,
        compiler_params=params,
        name="edges",
    )(*in_vmem(base, even1, odd1, coef))
    ahead = [(i, (i + 1) % ny_count) for i in range(ny_count)]
    back = [(j, i) for i, j in ahead]
    lo = lax.ppermute(high, "gy", ahead)
    hi = lax.ppermute(low, "gy", back)
    own = pl.pallas_call(
        functools.partial(first_kernel, ny),
        out_shape=pltpu.VMEM((-(-FIELDS * (ny + 2) // 8) * 8, nz), f32),
        in_specs=[vmem] * 7,
        out_specs=vmem,
        scratch_shapes=[pltpu.VMEM((3, FIELDS, ny + 16, nz), f32), pltpu.VMEM((10, ny + 16, nz), f32)],
        compiler_params=params,
        name="first_product",
    )(*in_vmem(scal, coef, lo, hi, base, even1, odd1))
    even2, odd2 = swap(own)
    shares = pl.pallas_call(
        functools.partial(second_kernel, ny, ny_count),
        out_shape=pltpu.VMEM((ny_count, 128), f32),
        in_specs=[vmem] * 10,
        out_specs=vmem,
        scratch_shapes=[pltpu.VMEM((3, FIELDS, ny + 8, nz), f32), pltpu.VMEM((ny + 8, nz), f32)],
        compiler_params=params,
        name="second_product",
    )(*in_vmem(scal, coef, lo, hi, base, even1, odd1, own, even2, odd2))
    shares = lax.all_to_all(shares, "gy", 0, 0, tiled=True)
    shares = jnp.broadcast_to(jnp.sum(shares, axis=0, keepdims=True), (nx_count, 128))
    shares = lax.all_to_all(shares, "gx", 0, 0, tiled=True)
    right, left = pl.pallas_call(
        functools.partial(last_kernel, ny),
        out_shape=[jax.ShapeDtypeStruct((comps * ny, nz), f32)] * 2,
        in_specs=[vmem] * 3,
        out_specs=[vmem] * 2,
        compiler_params=params,
        name="combine",
    )(*in_vmem(shares, base, own))
    return right.reshape(right_border.shape), left.reshape(left_border.shape)


def solution(mesh):
    block = P(None, "gx", "gy", None)
    return jax.shard_map(
        per_device,
        mesh=mesh,
        in_specs=(block, block, block, block, P(), P()),
        out_specs=(block, block),
        check_vma=False,
    )
```

```python
import functools

import jax
import jax.numpy as jnp
from jax import lax
from jax.experimental import pallas as pl
from jax.experimental.pallas import tpu as pltpu
from jax.sharding import PartitionSpec as P

CENTER = 8.0 / 3.0
EDGE = -1.0 / 6.0

COMPS = 5
FIELDS = 2 * COMPS
PLANE_ROWS = 2 * FIELDS + 1
SUMS = 5


def up(v):
    size = v.shape[-1]
    lane = lax.broadcasted_iota(jnp.int32, v.shape, v.ndim - 1)
    return jnp.where(lane == size - 1, 0.0, pltpu.roll(v, size - 1, v.ndim - 1))


def down(v):
    lane = lax.broadcasted_iota(jnp.int32, v.shape, v.ndim - 1)
    return jnp.where(lane == 0, 0.0, pltpu.roll(v, 1, v.ndim - 1))


def apply_both(mid, even, odd, vx, vy3, vz, vx_even, vx_odd, react, scal):
    number = lambda k: scal[k : k + 1]
    sign = number(COMPS * COMPS + COMPS)
    outs = []
    centers = [mid(f, 0) for f in range(FIELDS)]
    for f in range(FIELDS):
        c = f % COMPS
        right = f < COMPS
        b1, b0, b2 = centers[f], mid(f, -1), mid(f, 1)
        e1, o1 = even(f, 0), odd(f, 0)
        ya = (even(f, -1) + odd(f, -1)) + (even(f, 1) + odd(f, 1))
        t = (e1 + o1) + (b0 + b2) + 0.5 * ya
        d = number(COMPS * COMPS + c)
        base = (CENTER * d + react(c)) * b1
        if right:
            drift = (sign * vx) * (e1 - o1) + vy3[1] * (b2 - b0) + vz * (up(b1) - down(b1))
            out = base + (EDGE * d) * (ya + up(t) + down(t)) + 0.5 * drift
            for k in range(COMPS):
                out = out + number(c * COMPS + k) * centers[k]
        else:
            fz = 0.5 * (vz * b1)
            g = (EDGE * d) * t
            drift = sign * (vx_even * e1 - vx_odd * o1) + (vy3[2] * b2 - vy3[0] * b0)
            out = base + (EDGE * d) * ya - 0.5 * drift + up(g - fz) + down(g + fz)
            for k in range(COMPS):
                out = out + number(k * COMPS + c) * centers[COMPS + k]
        outs.append(out)
    return outs


def in_vmem(*arrays):
    return [pltpu.with_memory_space_constraint(v, pltpu.VMEM) for v in arrays]


def in_hbm(*arrays):
    return [pltpu.with_memory_space_constraint(v, pltpu.HBM) for v in arrays]


def numbers_kernel(coup_ref, diff_ref, scal):
    for k in range(COMPS * COMPS):
        scal[k : k + 1] = jnp.full((1, scal.shape[1]), coup_ref[k // COMPS, k % COMPS], jnp.float32)
    for c in range(COMPS):
        scal[COMPS * COMPS + c : COMPS * COMPS + c + 1] = jnp.full((1, scal.shape[1]), diff_ref[c], jnp.float32)
    sign = jnp.where(lax.rem(lax.axis_index("gx"), 2) == 0, 1.0, -1.0).astype(jnp.float32)
    last = COMPS * COMPS + COMPS
    scal[last : last + 1] = jnp.full((1, scal.shape[1]), sign, jnp.float32)


def load_kernel(ny, sr, sl, vel, rea, base, coef, sems):
    half = COMPS * ny
    copies = [
        pltpu.make_async_copy(src, dst, sems.at[k])
        for k, (src, dst) in enumerate(
            (
                (sr, base.at[0:half]),
                (sl, base.at[half : 2 * half]),
                (vel.at[0:ny], base.at[2 * half : 2 * half + ny]),
                (rea, coef.at[0:half]),
                (vel.at[ny : 3 * ny], coef.at[half : half + 2 * ny]),
            )
        )
    ]
    for copy in copies:
        copy.start()
    for copy in copies:
        copy.wait()


def edges_kernel(ny, base, even, odd, coef, low, high):
    for out, two, one in ((low, 0, 0), (high, ny - 2, ny - 1)):
        for plane, ref in enumerate((base, even, odd)):
            row = plane * PLANE_ROWS
            for f in range(FIELDS):
                out[row + 2 * f : row + 2 * f + 2] = ref[f * ny + two : f * ny + two + 2]
            at = FIELDS * ny + one
            out[row + 2 * FIELDS : row + 2 * FIELDS + 1] = ref[at : at + 1]
        row = 3 * PLANE_ROWS
        for c in range(COMPS + 1):
            at = (c if c < COMPS else COMPS + 1) * ny + one
            out[row + c : row + c + 1] = coef[at : at + 1]
        at = COMPS * ny + two
        out[row + COMPS + 1 : row + COMPS + 3] = coef[at : at + 2]


def first_kernel(ny, scal, coef, lo, hi, base, even, odd, out, field, cext):
    rows = ny + 8
    for side, ref in enumerate((base, even, odd)):
        at = side * PLANE_ROWS
        for f in range(FIELDS):
            field[side, f, 2 : ny + 2] = ref[f * ny : (f + 1) * ny]
            field[side, f, 0:2] = lo[at + 2 * f : at + 2 * f + 2]
            field[side, f, ny + 2 : ny + 4] = hi[at + 2 * f : at + 2 * f + 2]
    for c in range(9):
        if c < COMPS + 1:
            at, ref, row = (c if c < COMPS else COMPS + 1) * ny, coef, 3 * PLANE_ROWS + c
        else:
            at, ref, row = FIELDS * ny, (base, even, odd)[c - COMPS - 1], (c - COMPS) * PLANE_ROWS - 1
        cext[c, 1 : ny + 1] = ref[at : at + ny]
        cext[c, 0:1] = lo[row : row + 1]
        cext[c, ny + 1 : ny + 2] = hi[row : row + 1]
    row = 3 * PLANE_ROWS + COMPS + 1
    cext[9, 2 : ny + 2] = coef[COMPS * ny : (COMPS + 1) * ny]
    cext[9, 0:2] = lo[row : row + 2]
    cext[9, ny + 2 : ny + 4] = hi[row : row + 2]

    def plane(side):
        return lambda f, shift: field[side, f, 1 + shift : 1 + shift + rows]

    outs = apply_both(
        plane(0), plane(1), plane(2),
        cext[6, 0:rows], [cext[9, k : k + rows] for k in range(3)], cext[5, 0:rows],
        cext[7, 0:rows], cext[8, 0:rows], lambda c: cext[c, 0:rows], scal,
    )
    for f in range(FIELDS):
        field[0, f, 0:rows] = outs[f]
        out[f * ny : (f + 1) * ny] = field[0, f, 1 : ny + 1]
        at = FIELDS * ny + 2 * f
        out[at : at + 1] = field[0, f, 0:1]
        out[at + 1 : at + 2] = field[0, f, ny + 1 : ny + 2]


def second_kernel(ny, copies, scal, coef, lo, hi, base, even1, odd1, own, even, odd, out, field, vys):
    for f in range(FIELDS):
        for side, ref in ((0, own), (1, even), (2, odd)):
            field[side, f, 1 : ny + 1] = ref[f * ny : (f + 1) * ny]
            at = FIELDS * ny + 2 * f
            field[side, f, 0:1] = ref[at : at + 1]
            field[side, f, ny + 1 : ny + 2] = ref[at + 1 : at + 2]
    row = 3 * PLANE_ROWS + COMPS + 1
    vys[1 : ny + 1] = coef[COMPS * ny : (COMPS + 1) * ny]
    vys[0:1] = lo[row + 1 : row + 2]
    vys[ny + 1 : ny + 2] = hi[row : row + 1]

    def plane(side):
        ref = (own, even, odd)[side]
        return lambda f, shift: field[side, f, 1 + shift : 1 + shift + ny] if shift else ref[f * ny : (f + 1) * ny]

    at, vz = FIELDS * ny, (COMPS + 1) * ny
    outs = apply_both(
        plane(0), plane(1), plane(2),
        base[at : at + ny], [vys[k : k + ny] for k in range(3)], coef[vz : vz + ny],
        even1[at : at + ny], odd1[at : at + ny], lambda c: coef[c * ny : (c + 1) * ny], scal,
    )
    lane = lax.broadcasted_iota(jnp.int32, (1, 128), 1)
    total = jnp.zeros((1, 128), jnp.float32)
    for system in range(2):
        sums = [0.0] * SUMS
        for f in range(system * COMPS, (system + 1) * COMPS):
            s, w1, w2 = base[f * ny : (f + 1) * ny], own[f * ny : (f + 1) * ny], outs[f]
            for k, term in enumerate((w1 * w1, w1 * w2, w2 * w2, w1 * s, w2 * s)):
                sums[k] = sums[k] + term
        for k in range(SUMS):
            value = jnp.sum(jnp.sum(sums[k], axis=0, keepdims=True), axis=1, keepdims=True)
            total = total + jnp.where(lane == system * SUMS + k, value, 0.0)
    out[...] = jnp.broadcast_to(total, (copies, 128))


def last_kernel(ny, parts, base, own, out_r, out_l):
    total = jnp.sum(parts[...], axis=0, keepdims=True)
    lane = lax.broadcasted_iota(jnp.int32, (1, 128), 1)
    for system, out in ((0, out_r), (1, out_l)):
        g11, g12, g22, r1, r2 = [
            jnp.sum(jnp.where(lane == system * SUMS + k, total, 0.0), axis=1, keepdims=True)
            for k in range(SUMS)
        ]
        factor = g12 / g11
        b = (r2 - factor * r1) / (g22 - factor * g12)
        a = (r1 - g12 * b) / g11
        at = system * COMPS * ny
        out[...] = a * base[at : at + COMPS * ny] + b * own[at : at + COMPS * ny]


def per_device(right_border, left_border, velocity, reaction, diffusivity, coupling):
    comps, _, ny, nz = right_border.shape
    nx_count, ny_count = lax.axis_size("gx"), lax.axis_size("gy")
    f32 = jnp.float32
    params = pltpu.CompilerParams(vmem_limit_bytes=16 * 1024 * 1024)
    smem, vmem = pl.BlockSpec(memory_space=pltpu.SMEM), pl.BlockSpec(memory_space=pltpu.VMEM)
    sr, sl, vel, rea = (v.reshape(-1, nz) for v in (right_border, left_border, velocity, reaction))

    base, coef = pl.pallas_call(
        functools.partial(load_kernel, ny),
        out_shape=[pltpu.VMEM((rows * ny, nz), f32) for rows in (FIELDS + 1, COMPS + 2)],
        in_specs=[pl.BlockSpec(memory_space=pltpu.HBM)] * 4,
        out_specs=[vmem] * 2,
        scratch_shapes=[pltpu.SemaphoreType.DMA((5,))],
        compiler_params=params,
        name="load",
    )(*in_hbm(sr, sl, vel, rea))
    scal = pl.pallas_call(
        numbers_kernel,
        out_shape=pltpu.VMEM((32, nz), f32),
        in_specs=[smem] * 2,
        out_specs=vmem,
        compiler_params=params,
        name="numbers",
    )(coupling, diffusivity)

    even_pairs = [(i, i ^ 1) for i in range(nx_count)]
    odd_pairs = [(i, (i - 1 if i % 2 == 0 else i + 1) % nx_count) for i in range(nx_count)]

    def swap(v):
        odd = lax.ppermute(v, "gx", odd_pairs)
        return lax.ppermute(v, "gx", even_pairs), odd

    even1, odd1 = swap(base)
    low, high = pl.pallas_call(
        functools.partial(edges_kernel, ny),
        out_shape=[pltpu.VMEM((-(-(3 * PLANE_ROWS + COMPS + 3) // 8) * 8, nz), f32)] * 2,
        in_specs=[vmem] * 4,
        out_specs=[vmem] * 2,
        compiler_params=params,
        name="edges",
    )(*in_vmem(base, even1, odd1, coef))
    ahead = [(i, (i + 1) % ny_count) for i in range(ny_count)]
    back = [(j, i) for i, j in ahead]
    lo = lax.ppermute(high, "gy", ahead)
    hi = lax.ppermute(low, "gy", back)
    own = pl.pallas_call(
        functools.partial(first_kernel, ny),
        out_shape=pltpu.VMEM((-(-FIELDS * (ny + 2) // 8) * 8, nz), f32),
        in_specs=[vmem] * 7,
        out_specs=vmem,
        scratch_shapes=[pltpu.VMEM((3, FIELDS, ny + 16, nz), f32), pltpu.VMEM((10, ny + 16, nz), f32)],
        compiler_params=params,
        name="first_product",
    )(*in_vmem(scal, coef, lo, hi, base, even1, odd1))
    even2, odd2 = swap(own)
    shares = pl.pallas_call(
        functools.partial(second_kernel, ny, ny_count),
        out_shape=pltpu.VMEM((ny_count, 128), f32),
        in_specs=[vmem] * 10,
        out_specs=vmem,
        scratch_shapes=[pltpu.VMEM((3, FIELDS, ny + 8, nz), f32), pltpu.VMEM((ny + 8, nz), f32)],
        compiler_params=params,
        name="second_product",
    )(*in_vmem(scal, coef, lo, hi, base, even1, odd1, own, even2, odd2))
    shares = lax.all_to_all(shares, "gy", 0, 0, tiled=True)
    shares = jnp.broadcast_to(jnp.sum(shares, axis=0, keepdims=True), (nx_count, 128))
    shares = lax.all_to_all(shares, "gx", 0, 0, tiled=True)
    right, left = pl.pallas_call(
        functools.partial(last_kernel, ny),
        out_shape=[jax.ShapeDtypeStruct((comps * ny, nz), f32)] * 2,
        in_specs=[vmem] * 3,
        out_specs=[vmem] * 2,
        compiler_params=params,
        name="combine",
    )(*in_vmem(shares, base, own))
    return right.reshape(right_border.shape), left.reshape(left_border.shape)


def solution(mesh):
    block = P(None, "gx", "gy", None)
    return jax.shard_map(
        per_device,
        mesh=mesh,
        in_specs=(block, block, block, block, P(), P()),
        out_specs=(block, block),
        check_vma=False,
    )
```

```python
import functools

import jax
import jax.numpy as jnp
from jax import lax
from jax.experimental import pallas as pl
from jax.experimental.pallas import tpu as pltpu
from jax.sharding import PartitionSpec as P

CENTER = 8.0 / 3.0
EDGE = -1.0 / 6.0

COMPS = 5
SLABS_ALONG_Z = 8
FIELDS = 2 * COMPS
PLANE_ROWS = 2 * FIELDS + 1
SUMS = 5


def up(v):
    size = v.shape[-1]
    lane = lax.broadcasted_iota(jnp.int32, v.shape, v.ndim - 1)
    return jnp.where(lane == size - 1, 0.0, pltpu.roll(v, size - 1, v.ndim - 1))


def down(v):
    lane = lax.broadcasted_iota(jnp.int32, v.shape, v.ndim - 1)
    return jnp.where(lane == 0, 0.0, pltpu.roll(v, 1, v.ndim - 1))


def apply_both(mid, even, odd, vx, vy3, vz, vx_even, vx_odd, react, scal):
    number = lambda k: scal[k : k + 1]
    sign = number(COMPS * COMPS + COMPS)
    outs = []
    centers = [mid(f, 0) for f in range(FIELDS)]
    for f in range(FIELDS):
        c = f % COMPS
        right = f < COMPS
        b1, b0, b2 = centers[f], mid(f, -1), mid(f, 1)
        e1, o1 = even(f, 0), odd(f, 0)
        ya = (even(f, -1) + odd(f, -1)) + (even(f, 1) + odd(f, 1))
        t = (e1 + o1) + (b0 + b2) + 0.5 * ya
        d = number(COMPS * COMPS + c)
        base = (CENTER * d + react(c)) * b1
        if right:
            drift = (sign * vx) * (e1 - o1) + vy3[1] * (b2 - b0) + vz * (up(b1) - down(b1))
            out = base + (EDGE * d) * (ya + up(t) + down(t)) + 0.5 * drift
            for k in range(COMPS):
                out = out + number(c * COMPS + k) * centers[k]
        else:
            fz = 0.5 * (vz * b1)
            g = (EDGE * d) * t
            drift = sign * (vx_even * e1 - vx_odd * o1) + (vy3[2] * b2 - vy3[0] * b0)
            out = base + (EDGE * d) * ya - 0.5 * drift + up(g - fz) + down(g + fz)
            for k in range(COMPS):
                out = out + number(k * COMPS + c) * centers[COMPS + k]
        outs.append(out)
    return outs


def in_vmem(*arrays):
    return [pltpu.with_memory_space_constraint(v, pltpu.VMEM) for v in arrays]


def in_hbm(*arrays):
    return [pltpu.with_memory_space_constraint(v, pltpu.HBM) for v in arrays]


def numbers_kernel(coup_ref, diff_ref, scal):
    for k in range(COMPS * COMPS):
        scal[k : k + 1] = jnp.full((1, scal.shape[1]), coup_ref[k // COMPS, k % COMPS], jnp.float32)
    for c in range(COMPS):
        scal[COMPS * COMPS + c : COMPS * COMPS + c + 1] = jnp.full((1, scal.shape[1]), diff_ref[c], jnp.float32)
    sign = jnp.where(lax.rem(lax.axis_index("gx"), 2) == 0, 1.0, -1.0).astype(jnp.float32)
    last = COMPS * COMPS + COMPS
    scal[last : last + 1] = jnp.full((1, scal.shape[1]), sign, jnp.float32)


def load_kernel(ny, sr, sl, vel, rea, base, coef, sems):
    half = COMPS * ny
    copies = [
        pltpu.make_async_copy(src, dst, sems.at[k])
        for k, (src, dst) in enumerate(
            (
                (sr, base.at[0:half]),
                (sl, base.at[half : 2 * half]),
                (vel.at[0:ny], base.at[2 * half : 2 * half + ny]),
                (rea, coef.at[0:half]),
                (vel.at[ny : 3 * ny], coef.at[half : half + 2 * ny]),
            )
        )
    ]
    for copy in copies:
        copy.start()
    for copy in copies:
        copy.wait()


def edges_kernel(ny, base, even, odd, coef, low, high):
    for out, two, one in ((low, 0, 0), (high, ny - 2, ny - 1)):
        for plane, ref in enumerate((base, even, odd)):
            row = plane * PLANE_ROWS
            for f in range(FIELDS):
                out[row + 2 * f : row + 2 * f + 2] = ref[f * ny + two : f * ny + two + 2]
            at = FIELDS * ny + one
            out[row + 2 * FIELDS : row + 2 * FIELDS + 1] = ref[at : at + 1]
        row = 3 * PLANE_ROWS
        for c in range(COMPS + 1):
            at = (c if c < COMPS else COMPS + 1) * ny + one
            out[row + c : row + c + 1] = coef[at : at + 1]
        at = COMPS * ny + two
        out[row + COMPS + 1 : row + COMPS + 3] = coef[at : at + 2]


def first_kernel(ny, scal, coef, lo, hi, base, even, odd, out, field, cext):
    rows = ny + 8
    for side, ref in enumerate((base, even, odd)):
        at = side * PLANE_ROWS
        for f in range(FIELDS):
            field[side, f, 2 : ny + 2] = ref[f * ny : (f + 1) * ny]
            field[side, f, 0:2] = lo[at + 2 * f : at + 2 * f + 2]
            field[side, f, ny + 2 : ny + 4] = hi[at + 2 * f : at + 2 * f + 2]
    for c in range(9):
        if c < COMPS + 1:
            at, ref, row = (c if c < COMPS else COMPS + 1) * ny, coef, 3 * PLANE_ROWS + c
        else:
            at, ref, row = FIELDS * ny, (base, even, odd)[c - COMPS - 1], (c - COMPS) * PLANE_ROWS - 1
        cext[c, 1 : ny + 1] = ref[at : at + ny]
        cext[c, 0:1] = lo[row : row + 1]
        cext[c, ny + 1 : ny + 2] = hi[row : row + 1]
    row = 3 * PLANE_ROWS + COMPS + 1
    cext[9, 2 : ny + 2] = coef[COMPS * ny : (COMPS + 1) * ny]
    cext[9, 0:2] = lo[row : row + 2]
    cext[9, ny + 2 : ny + 4] = hi[row : row + 2]

    def plane(side):
        return lambda f, shift: field[side, f, 1 + shift : 1 + shift + rows]

    outs = apply_both(
        plane(0), plane(1), plane(2),
        cext[6, 0:rows], [cext[9, k : k + rows] for k in range(3)], cext[5, 0:rows],
        cext[7, 0:rows], cext[8, 0:rows], lambda c: cext[c, 0:rows], scal,
    )
    for f in range(FIELDS):
        field[0, f, 0:rows] = outs[f]
        out[f * ny : (f + 1) * ny] = field[0, f, 1 : ny + 1]
        at = FIELDS * ny + 2 * f
        out[at : at + 1] = field[0, f, 0:1]
        out[at + 1 : at + 2] = field[0, f, ny + 1 : ny + 2]


def second_kernel(ny, copies, scal, coef, lo, hi, base, even1, odd1, own, even, odd, out, field, vys):
    for f in range(FIELDS):
        for side, ref in ((0, own), (1, even), (2, odd)):
            field[side, f, 1 : ny + 1] = ref[f * ny : (f + 1) * ny]
            at = FIELDS * ny + 2 * f
            field[side, f, 0:1] = ref[at : at + 1]
            field[side, f, ny + 1 : ny + 2] = ref[at + 1 : at + 2]
    row = 3 * PLANE_ROWS + COMPS + 1
    vys[1 : ny + 1] = coef[COMPS * ny : (COMPS + 1) * ny]
    vys[0:1] = lo[row + 1 : row + 2]
    vys[ny + 1 : ny + 2] = hi[row : row + 1]

    def plane(side):
        ref = (own, even, odd)[side]
        return lambda f, shift: field[side, f, 1 + shift : 1 + shift + ny] if shift else ref[f * ny : (f + 1) * ny]

    at, vz = FIELDS * ny, (COMPS + 1) * ny
    outs = apply_both(
        plane(0), plane(1), plane(2),
        base[at : at + ny], [vys[k : k + ny] for k in range(3)], coef[vz : vz + ny],
        even1[at : at + ny], odd1[at : at + ny], lambda c: coef[c * ny : (c + 1) * ny], scal,
    )
    lane = lax.broadcasted_iota(jnp.int32, (1, 128), 1)
    total = jnp.zeros((1, 128), jnp.float32)
    for system in range(2):
        sums = [0.0] * SUMS
        for f in range(system * COMPS, (system + 1) * COMPS):
            s, w1, w2 = base[f * ny : (f + 1) * ny], own[f * ny : (f + 1) * ny], outs[f]
            for k, term in enumerate((w1 * w1, w1 * w2, w2 * w2, w1 * s, w2 * s)):
                sums[k] = sums[k] + term
        for k in range(SUMS):
            value = jnp.sum(jnp.sum(sums[k], axis=0, keepdims=True), axis=1, keepdims=True)
            total = total + jnp.where(lane == system * SUMS + k, value, 0.0)
    out[...] = jnp.broadcast_to(total, (copies, 128))


def last_kernel(ny, parts, base, own, out_r, out_l):
    total = jnp.sum(parts[...], axis=0, keepdims=True)
    lane = lax.broadcasted_iota(jnp.int32, (1, 128), 1)
    for system, out in ((0, out_r), (1, out_l)):
        g11, g12, g22, r1, r2 = [
            jnp.sum(jnp.where(lane == system * SUMS + k, total, 0.0), axis=1, keepdims=True)
            for k in range(SUMS)
        ]
        factor = g12 / g11
        b = (r2 - factor * r1) / (g22 - factor * g12)
        a = (r1 - g12 * b) / g11
        at = system * COMPS * ny
        out[...] = a * base[at : at + COMPS * ny] + b * own[at : at + COMPS * ny]


def per_device(right_border, left_border, velocity, reaction, diffusivity, coupling):
    comps, _, ny, nz = right_border.shape
    nx_count, ny_count = lax.axis_size("gx"), lax.axis_size("gy")
    f32 = jnp.float32
    params = pltpu.CompilerParams(vmem_limit_bytes=16 * 1024 * 1024)
    smem, vmem = pl.BlockSpec(memory_space=pltpu.SMEM), pl.BlockSpec(memory_space=pltpu.VMEM)
    sr, sl, vel, rea = (v.reshape(-1, nz) for v in (right_border, left_border, velocity, reaction))

    base, coef = pl.pallas_call(
        functools.partial(load_kernel, ny),
        out_shape=[pltpu.VMEM((rows * ny, nz), f32) for rows in (FIELDS + 1, COMPS + 2)],
        in_specs=[pl.BlockSpec(memory_space=pltpu.HBM)] * 4,
        out_specs=[vmem] * 2,
        scratch_shapes=[pltpu.SemaphoreType.DMA((5,))],
        compiler_params=params,
        name="load",
    )(*in_hbm(sr, sl, vel, rea))
    scal = pl.pallas_call(
        numbers_kernel,
        out_shape=pltpu.VMEM((32, nz), f32),
        in_specs=[smem] * 2,
        out_specs=vmem,
        compiler_params=params,
        name="numbers",
    )(coupling, diffusivity)

    even_pairs = [(i, i ^ 1) for i in range(nx_count)]
    odd_pairs = [(i, (i - 1 if i % 2 == 0 else i + 1) % nx_count) for i in range(nx_count)]

    def swap(v):
        odd = lax.ppermute(v, "gx", odd_pairs)
        return lax.ppermute(v, "gx", even_pairs), odd

    even1, odd1 = swap(base)
    low, high = pl.pallas_call(
        functools.partial(edges_kernel, ny),
        out_shape=[pltpu.VMEM((-(-(3 * PLANE_ROWS + COMPS + 3) // 8) * 8, nz), f32)] * 2,
        in_specs=[vmem] * 4,
        out_specs=[vmem] * 2,
        compiler_params=params,
        name="edges",
    )(*in_vmem(base, even1, odd1, coef))
    ahead = [(i, (i + 1) % ny_count) for i in range(ny_count)]
    back = [(j, i) for i, j in ahead]
    lo = lax.ppermute(high, "gy", ahead)
    hi = lax.ppermute(low, "gy", back)
    own = pl.pallas_call(
        functools.partial(first_kernel, ny),
        out_shape=pltpu.VMEM((-(-FIELDS * (ny + 2) // 8) * 8, nz), f32),
        in_specs=[vmem] * 7,
        out_specs=vmem,
        scratch_shapes=[pltpu.VMEM((3, FIELDS, ny + 16, nz), f32), pltpu.VMEM((10, ny + 16, nz), f32)],
        compiler_params=params,
        name="first_product",
    )(*in_vmem(scal, coef, lo, hi, base, even1, odd1))
    even2, odd2 = swap(own)
    shares = pl.pallas_call(
        functools.partial(second_kernel, ny, ny_count),
        out_shape=pltpu.VMEM((ny_count, 128), f32),
        in_specs=[vmem] * 10,
        out_specs=vmem,
        scratch_shapes=[pltpu.VMEM((3, FIELDS, ny + 8, nz), f32), pltpu.VMEM((ny + 8, nz), f32)],
        compiler_params=params,
        name="second_product",
    )(*in_vmem(scal, coef, lo, hi, base, even1, odd1, own, even2, odd2))
    slabs = sorted(range(nx_count), key=lambda g: (-(g % SLABS_ALONG_Z), abs(g // SLABS_ALONG_Z - SLABS_ALONG_Z // 2)))
    strips = sorted(range(ny_count), key=lambda g: (5, 7, 3, 4, 6, 1, 2, 0).index(g)) if ny_count == 8 else list(range(ny_count))
    shares = lax.all_to_all(shares, "gy", 0, 0, tiled=True, axis_index_groups=[strips])
    shares = jnp.broadcast_to(jnp.sum(shares, axis=0, keepdims=True), (nx_count, 128))
    shares = lax.all_to_all(shares, "gx", 0, 0, tiled=True, axis_index_groups=[slabs])
    right, left = pl.pallas_call(
        functools.partial(last_kernel, ny),
        out_shape=[jax.ShapeDtypeStruct((comps * ny, nz), f32)] * 2,
        in_specs=[vmem] * 3,
        out_specs=[vmem] * 2,
        compiler_params=params,
        name="combine",
    )(*in_vmem(shares, base, own))
    return right.reshape(right_border.shape), left.reshape(left_border.shape)


def solution(mesh):
    block = P(None, "gx", "gy", None)
    return jax.shard_map(
        per_device,
        mesh=mesh,
        in_specs=(block, block, block, block, P(), P()),
        out_specs=(block, block),
        check_vma=False,
    )
```

```python
import functools

import jax
import jax.numpy as jnp
from jax import lax
from jax.experimental import pallas as pl
from jax.experimental.pallas import tpu as pltpu
from jax.sharding import PartitionSpec as P

CENTER = 8.0 / 3.0
EDGE = -1.0 / 6.0

COMPS = 5
SLABS_ALONG_Z = 8
FIELDS = 2 * COMPS
PLANE_ROWS = 2 * FIELDS + 1
SUMS = 5


def up(v):
    size = v.shape[-1]
    lane = lax.broadcasted_iota(jnp.int32, v.shape, v.ndim - 1)
    return jnp.where(lane == size - 1, 0.0, pltpu.roll(v, size - 1, v.ndim - 1))


def down(v):
    lane = lax.broadcasted_iota(jnp.int32, v.shape, v.ndim - 1)
    return jnp.where(lane == 0, 0.0, pltpu.roll(v, 1, v.ndim - 1))


def apply_both(mid, even, odd, vx, vy3, vz, vx_even, vx_odd, react, scal):
    number = lambda k: scal[k : k + 1]
    sign = number(COMPS * COMPS + COMPS)
    outs = []
    centers = [mid(f, 0) for f in range(FIELDS)]
    for f in range(FIELDS):
        c = f % COMPS
        right = f < COMPS
        b1, b0, b2 = centers[f], mid(f, -1), mid(f, 1)
        e1, o1 = even(f, 0), odd(f, 0)
        ya = (even(f, -1) + odd(f, -1)) + (even(f, 1) + odd(f, 1))
        t = (e1 + o1) + (b0 + b2) + 0.5 * ya
        d = number(COMPS * COMPS + c)
        base = (CENTER * d + react(c)) * b1
        if right:
            drift = (sign * vx) * (e1 - o1) + vy3[1] * (b2 - b0) + vz * (up(b1) - down(b1))
            out = base + (EDGE * d) * (ya + up(t) + down(t)) + 0.5 * drift
            for k in range(COMPS):
                out = out + number(c * COMPS + k) * centers[k]
        else:
            fz = 0.5 * (vz * b1)
            g = (EDGE * d) * t
            drift = sign * (vx_even * e1 - vx_odd * o1) + (vy3[2] * b2 - vy3[0] * b0)
            out = base + (EDGE * d) * ya - 0.5 * drift + up(g - fz) + down(g + fz)
            for k in range(COMPS):
                out = out + number(k * COMPS + c) * centers[COMPS + k]
        outs.append(out)
    return outs


def in_vmem(*arrays):
    return [pltpu.with_memory_space_constraint(v, pltpu.VMEM) for v in arrays]


def in_hbm(*arrays):
    return [pltpu.with_memory_space_constraint(v, pltpu.HBM) for v in arrays]


def numbers_kernel(coup_ref, diff_ref, scal):
    for k in range(COMPS * COMPS):
        scal[k : k + 1] = jnp.full((1, scal.shape[1]), coup_ref[k // COMPS, k % COMPS], jnp.float32)
    for c in range(COMPS):
        scal[COMPS * COMPS + c : COMPS * COMPS + c + 1] = jnp.full((1, scal.shape[1]), diff_ref[c], jnp.float32)
    sign = jnp.where(lax.rem(lax.axis_index("gx"), 2) == 0, 1.0, -1.0).astype(jnp.float32)
    last = COMPS * COMPS + COMPS
    scal[last : last + 1] = jnp.full((1, scal.shape[1]), sign, jnp.float32)


def load_kernel(ny, sr, sl, vel, rea, base, coef, sems):
    half = COMPS * ny
    copies = [
        pltpu.make_async_copy(src, dst, sems.at[k])
        for k, (src, dst) in enumerate(
            (
                (sr, base.at[0:half]),
                (sl, base.at[half : 2 * half]),
                (vel.at[0:ny], base.at[2 * half : 2 * half + ny]),
                (rea, coef.at[0:half]),
                (vel.at[ny : 3 * ny], coef.at[half : half + 2 * ny]),
            )
        )
    ]
    for copy in copies:
        copy.start()
    for copy in copies:
        copy.wait()


def edges_kernel(ny, base, even, odd, coef, low, high):
    for out, two, one in ((low, 0, 0), (high, ny - 2, ny - 1)):
        for plane, ref in enumerate((base, even, odd)):
            row = plane * PLANE_ROWS
            for f in range(FIELDS):
                out[row + 2 * f : row + 2 * f + 2] = ref[f * ny + two : f * ny + two + 2]
            at = FIELDS * ny + one
            out[row + 2 * FIELDS : row + 2 * FIELDS + 1] = ref[at : at + 1]
        row = 3 * PLANE_ROWS
        for c in range(COMPS + 1):
            at = (c if c < COMPS else COMPS + 1) * ny + one
            out[row + c : row + c + 1] = coef[at : at + 1]
        at = COMPS * ny + two
        out[row + COMPS + 1 : row + COMPS + 3] = coef[at : at + 2]


def first_kernel(ny, scal, coef, lo, hi, base, even, odd, out, field, cext):
    rows = ny + 8
    for side, ref in enumerate((base, even, odd)):
        at = side * PLANE_ROWS
        for f in range(FIELDS):
            field[side, f, 2 : ny + 2] = ref[f * ny : (f + 1) * ny]
            field[side, f, 0:2] = lo[at + 2 * f : at + 2 * f + 2]
            field[side, f, ny + 2 : ny + 4] = hi[at + 2 * f : at + 2 * f + 2]
    for c in range(9):
        if c < COMPS + 1:
            at, ref, row = (c if c < COMPS else COMPS + 1) * ny, coef, 3 * PLANE_ROWS + c
        else:
            at, ref, row = FIELDS * ny, (base, even, odd)[c - COMPS - 1], (c - COMPS) * PLANE_ROWS - 1
        cext[c, 1 : ny + 1] = ref[at : at + ny]
        cext[c, 0:1] = lo[row : row + 1]
        cext[c, ny + 1 : ny + 2] = hi[row : row + 1]
    row = 3 * PLANE_ROWS + COMPS + 1
    cext[9, 2 : ny + 2] = coef[COMPS * ny : (COMPS + 1) * ny]
    cext[9, 0:2] = lo[row : row + 2]
    cext[9, ny + 2 : ny + 4] = hi[row : row + 2]

    def plane(side):
        return lambda f, shift: field[side, f, 1 + shift : 1 + shift + rows]

    outs = apply_both(
        plane(0), plane(1), plane(2),
        cext[6, 0:rows], [cext[9, k : k + rows] for k in range(3)], cext[5, 0:rows],
        cext[7, 0:rows], cext[8, 0:rows], lambda c: cext[c, 0:rows], scal,
    )
    for f in range(FIELDS):
        field[0, f, 0:rows] = outs[f]
        out[f * ny : (f + 1) * ny] = field[0, f, 1 : ny + 1]
        at = FIELDS * ny + 2 * f
        out[at : at + 1] = field[0, f, 0:1]
        out[at + 1 : at + 2] = field[0, f, ny + 1 : ny + 2]


def second_kernel(ny, copies, scal, coef, lo, hi, base, even1, odd1, own, even, odd, out, field, vys):
    for f in range(FIELDS):
        at, block = FIELDS * ny + 2 * f, slice(f * ny, (f + 1) * ny)
        field[0, f, 1 : ny + 1] = own[block]
        field[0, f, 0:1] = own[at : at + 1]
        field[0, f, ny + 1 : ny + 2] = own[at + 1 : at + 2]
        field[1, f, 1 : ny + 1] = even[block] + odd[block]
        field[1, f, 0:1] = even[at : at + 1] + odd[at : at + 1]
        field[1, f, ny + 1 : ny + 2] = even[at + 1 : at + 2] + odd[at + 1 : at + 2]
    row = 3 * PLANE_ROWS + COMPS + 1
    vys[1 : ny + 1] = coef[COMPS * ny : (COMPS + 1) * ny]
    vys[0:1] = lo[row + 1 : row + 2]
    vys[ny + 1 : ny + 2] = hi[row : row + 1]

    def plane(side):
        ref = (own, even, odd)[side]
        if side == 2:
            return lambda f, shift: 0.0 if shift else ref[f * ny : (f + 1) * ny]
        return lambda f, shift: field[side, f, 1 + shift : 1 + shift + ny] if shift else ref[f * ny : (f + 1) * ny]

    at, vz = FIELDS * ny, (COMPS + 1) * ny
    outs = apply_both(
        plane(0), plane(1), plane(2),
        base[at : at + ny], [vys[k : k + ny] for k in range(3)], coef[vz : vz + ny],
        even1[at : at + ny], odd1[at : at + ny], lambda c: coef[c * ny : (c + 1) * ny], scal,
    )
    lane = lax.broadcasted_iota(jnp.int32, (1, 128), 1)
    total = jnp.zeros((1, 128), jnp.float32)
    for system in range(2):
        sums = [0.0] * SUMS
        for f in range(system * COMPS, (system + 1) * COMPS):
            s, w1, w2 = base[f * ny : (f + 1) * ny], own[f * ny : (f + 1) * ny], outs[f]
            for k, term in enumerate((w1 * w1, w1 * w2, w2 * w2, w1 * s, w2 * s)):
                sums[k] = sums[k] + term
        for k in range(SUMS):
            value = jnp.sum(jnp.sum(sums[k], axis=0, keepdims=True), axis=1, keepdims=True)
            total = total + jnp.where(lane == system * SUMS + k, value, 0.0)
    out[...] = jnp.broadcast_to(total, (copies, 128))


def last_kernel(ny, parts, base, own, out_r, out_l):
    total = jnp.sum(parts[...], axis=0, keepdims=True)
    lane = lax.broadcasted_iota(jnp.int32, (1, 128), 1)
    for system, out in ((0, out_r), (1, out_l)):
        g11, g12, g22, r1, r2 = [
            jnp.sum(jnp.where(lane == system * SUMS + k, total, 0.0), axis=1, keepdims=True)
            for k in range(SUMS)
        ]
        factor = g12 / g11
        b = (r2 - factor * r1) / (g22 - factor * g12)
        a = (r1 - g12 * b) / g11
        at = system * COMPS * ny
        out[...] = a * base[at : at + COMPS * ny] + b * own[at : at + COMPS * ny]


def per_device(right_border, left_border, velocity, reaction, diffusivity, coupling):
    comps, _, ny, nz = right_border.shape
    nx_count, ny_count = lax.axis_size("gx"), lax.axis_size("gy")
    f32 = jnp.float32
    params = pltpu.CompilerParams(vmem_limit_bytes=16 * 1024 * 1024)
    smem, vmem = pl.BlockSpec(memory_space=pltpu.SMEM), pl.BlockSpec(memory_space=pltpu.VMEM)
    sr, sl, vel, rea = (v.reshape(-1, nz) for v in (right_border, left_border, velocity, reaction))

    base, coef = pl.pallas_call(
        functools.partial(load_kernel, ny),
        out_shape=[pltpu.VMEM((rows * ny, nz), f32) for rows in (FIELDS + 1, COMPS + 2)],
        in_specs=[pl.BlockSpec(memory_space=pltpu.HBM)] * 4,
        out_specs=[vmem] * 2,
        scratch_shapes=[pltpu.SemaphoreType.DMA((5,))],
        compiler_params=params,
        name="load",
    )(*in_hbm(sr, sl, vel, rea))
    scal = pl.pallas_call(
        numbers_kernel,
        out_shape=pltpu.VMEM((32, nz), f32),
        in_specs=[smem] * 2,
        out_specs=vmem,
        compiler_params=params,
        name="numbers",
    )(coupling, diffusivity)

    even_pairs = [(i, i ^ 1) for i in range(nx_count)]
    odd_pairs = [(i, (i - 1 if i % 2 == 0 else i + 1) % nx_count) for i in range(nx_count)]

    def swap(v):
        odd = lax.ppermute(v, "gx", odd_pairs)
        return lax.ppermute(v, "gx", even_pairs), odd

    even1, odd1 = swap(base)
    low, high = pl.pallas_call(
        functools.partial(edges_kernel, ny),
        out_shape=[pltpu.VMEM((-(-(3 * PLANE_ROWS + COMPS + 3) // 8) * 8, nz), f32)] * 2,
        in_specs=[vmem] * 4,
        out_specs=[vmem] * 2,
        compiler_params=params,
        name="edges",
    )(*in_vmem(base, even1, odd1, coef))
    ahead = [(i, (i + 1) % ny_count) for i in range(ny_count)]
    back = [(j, i) for i, j in ahead]
    lo = lax.ppermute(high, "gy", ahead)
    hi = lax.ppermute(low, "gy", back)
    own = pl.pallas_call(
        functools.partial(first_kernel, ny),
        out_shape=pltpu.VMEM((-(-FIELDS * (ny + 2) // 8) * 8, nz), f32),
        in_specs=[vmem] * 7,
        out_specs=vmem,
        scratch_shapes=[pltpu.VMEM((3, FIELDS, ny + 16, nz), f32), pltpu.VMEM((10, ny + 16, nz), f32)],
        compiler_params=params,
        name="first_product",
    )(*in_vmem(scal, coef, lo, hi, base, even1, odd1))
    even2, odd2 = swap(own)
    shares = pl.pallas_call(
        functools.partial(second_kernel, ny, ny_count),
        out_shape=pltpu.VMEM((ny_count, 128), f32),
        in_specs=[vmem] * 10,
        out_specs=vmem,
        scratch_shapes=[pltpu.VMEM((2, FIELDS, ny + 8, nz), f32), pltpu.VMEM((ny + 8, nz), f32)],
        compiler_params=params,
        name="second_product",
    )(*in_vmem(scal, coef, lo, hi, base, even1, odd1, own, even2, odd2))
    slabs = sorted(range(nx_count), key=lambda g: (-(g % SLABS_ALONG_Z), abs(g // SLABS_ALONG_Z - SLABS_ALONG_Z // 2)))
    strips = sorted(range(ny_count), key=lambda g: (5, 7, 3, 4, 6, 1, 2, 0).index(g)) if ny_count == 8 else list(range(ny_count))
    shares = lax.all_to_all(shares, "gy", 0, 0, tiled=True, axis_index_groups=[strips])
    shares = jnp.broadcast_to(jnp.sum(shares, axis=0, keepdims=True), (nx_count, 128))
    shares = lax.all_to_all(shares, "gx", 0, 0, tiled=True, axis_index_groups=[slabs])
    right, left = pl.pallas_call(
        functools.partial(last_kernel, ny),
        out_shape=[jax.ShapeDtypeStruct((comps * ny, nz), f32)] * 2,
        in_specs=[vmem] * 3,
        out_specs=[vmem] * 2,
        compiler_params=params,
        name="combine",
    )(*in_vmem(shares, base, own))
    return right.reshape(right_border.shape), left.reshape(left_border.shape)


def solution(mesh):
    block = P(None, "gx", "gy", None)
    return jax.shard_map(
        per_device,
        mesh=mesh,
        in_specs=(block, block, block, block, P(), P()),
        out_specs=(block, block),
        check_vma=False,
    )
```
